128 devices in a mesh: tm: 8 (over z, y_lo), tmpl: 16 (over y_hi, x, core).
Axes of the slice: x: 4, y: 4 (y_hi: 2, y_lo: 2; y = y_hi * 2 + y_lo), z: 4, core: 2. Of those that a mesh axis runs over, the one named last changes fastest.
Arguments:
- strain: float32 [16, 262144], P('tmpl', 'tm'), may hold values from -6 to 6
- psd_bins: int32 [8, 65536], P(None, 'tmpl'), may hold values from 0 to 8191, as said below
- psd_values: float32 [8, 8192], P('tm'), may hold values from 0.25 to 4
- chirp_slope: int32 [32], P('tmpl'), may hold values from 0 to 1023
- chirp_curve: int32 [32], P('tmpl'), may hold values from 1 to 63
Outputs:
- snr: float32 [32, 4194304], P('tmpl', 'tm')
The draws below stay inside these ranges and needn't reach their ends.
Inputs may be any that keep to these rules, and one draw needn't show every extreme that they name: psd_bins[r, c] names the row of psd_values that serves frequency bin r * 65536 + c.
All inputs are finite; a program needn't handle non-finite values.
Results may differ from the reference program's by a relative error of at most 0.0003.
Values sent between devices are 32-bit elements; how exact they have to be, the bound alone decides.
No kernel may reach another device: no remote copies, remote signals or barrier semaphores. Data moves between devices by JAX's collectives and lax.ppermute only.
A program may use at most 128 MiB of HBM per device.

```python
import math
import jax
import jax.numpy as jnp
from jax import lax

SUB = 65536
OR = 32768
R = 8192
LANES = 16
SEGMENTS = 8
ROWS = 32768
HALF_ROWS = 8
TEMPLATES = 32


def draw_psd_bins(key, part):
    frequency = jnp.arange(HALF_ROWS * SUB, dtype=jnp.int32)
    base_row = frequency // (HALF_ROWS * SUB // R)
    jitter = jax.random.randint(key, frequency.shape, 0, 2, dtype=jnp.int32)
    jitter = jnp.where(frequency == 0, 0, jitter)
    return jnp.minimum(base_row + jitter, R - 1).reshape(HALF_ROWS, SUB)


def place_ends(entries, rng, smallest, high):
    extent = entries.shape
    spot = [jax.random.randint(jax.random.fold_in(rng, axis), (), 0, extent[axis]) for axis in range(len(extent))]
    entries = entries.at[tuple(spot)].set(smallest)
    longest = extent.index(max(extent))
    spot[longest] = (spot[longest] + 1) % extent[longest]
    return entries.at[tuple(spot)].set(high)


def block_scale(own_key, shape, pieces, smallest, largest):
    factor_of = 1.0
    for dim, shards_of in pieces:
        draws = jax.random.uniform(jax.random.fold_in(jax.random.fold_in(own_key, 6), dim), (shards_of,), jnp.float32, smallest / len(pieces), largest / len(pieces))
        factor_of = factor_of * jnp.repeat(jnp.exp(draws), shape[dim] // shards_of).reshape((-1,) + (1,) * (len(shape) - 1 - dim))
    return factor_of


def centred(key, shape, scale, bound, cuts=(), kind=jnp.bfloat16):
    loudness = block_scale(key, shape, cuts, -0.22, 0.18) if cuts else 1.0
    drawn = jax.random.normal(key, shape, jnp.float32) * scale * loudness
    return jnp.minimum(jnp.maximum(drawn, -bound), bound).astype(kind)


def setup_inputs(seed: int = 0) -> dict:
    splits = jax.random.split(jax.random.key(seed), 6)
    strain = centred(splits[0], (LANES, SEGMENTS * ROWS), 1.0, 6.0, ((0, 16), (1, 8)), jnp.float32)
    psd_bins = draw_psd_bins(jax.random.fold_in(splits[5], 71), 0)
    psd_values = jnp.clip(jnp.exp(math.log(4.0) - 2.7725887 * jax.random.uniform(splits[2], (SEGMENTS, R), jnp.float32) ** block_scale(splits[2], (SEGMENTS, R), ((0, 8),), -0.2, 0.2)), 0.25, 4.0)
    chirp_slope = place_ends(jax.random.randint(splits[3], (TEMPLATES,), 0, 1024), jax.random.fold_in(splits[3], 1), 0, 1023).astype(jnp.int32)
    chirp_curve = place_ends(jax.random.randint(splits[4], (TEMPLATES,), 1, 64), jax.random.fold_in(splits[4], 1), 1, 63).astype(jnp.int32)
    return {"strain": strain, "psd_bins": psd_bins, "psd_values": psd_values, "chirp_slope": chirp_slope, "chirp_curve": chirp_curve}


TWO_PI = 2.0 * math.pi

def chirp_phase(frequency, slope, curve, modulus):
    high_part = frequency // 1024
    low_part = frequency % 1024
    square = 2 * high_part * low_part % (modulus // 1024) * 1024 + low_part * low_part
    square = square % modulus
    return (slope * frequency + curve * square) % modulus

def template_parts(frequency, chirp_slope, chirp_curve, modulus, k_low, k_cut):
    phase = chirp_phase(frequency[None, :], chirp_slope[:, None], chirp_curve[:, None], modulus)
    angles = phase.astype(jnp.float32) * (TWO_PI / modulus)
    ratio = frequency.astype(jnp.float32) / k_low
    inside = (frequency >= k_low) & (frequency < k_cut)
    amplitude = jnp.where(inside, jnp.power(jnp.maximum(ratio, 1.0), -7.0 / 6.0), 0.0)
    return (amplitude * jnp.cos(angles), -amplitude * jnp.sin(angles))

def reference(strain, psd_bins, psd_values, chirp_slope, chirp_curve):
    lanes = strain.shape[0]
    total_len = SUB * lanes
    half_len = total_len // 2
    intersection = OR * lanes
    stride = ROWS * lanes
    stream = strain.T.reshape(-1)
    padded = jnp.concatenate([jnp.zeros((intersection,), jnp.float32), stream])
    frequency = jnp.arange(half_len, dtype=jnp.int32)
    tmpl_re, tmpl_im = template_parts(frequency, chirp_slope, chirp_curve, total_len, total_len // 200, 3 * total_len // 8)
    power = tmpl_re * tmpl_re + tmpl_im * tmpl_im
    bins = psd_bins.reshape(-1)
    norm_scale = 1.0 / math.sqrt(total_len)

    def one_segment(segment):
        start = (segment * stride).astype(jnp.int32)
        data = lax.dynamic_slice(padded, (start,), (total_len,))
        spectrum = jnp.fft.fft(data)[:half_len]
        inv_psd = 1.0 / jnp.take(psd_values[segment], bins)
        white_re = jnp.real(spectrum) * inv_psd * norm_scale
        white_im = jnp.imag(spectrum) * inv_psd * norm_scale
        coef_re = white_re * tmpl_re + white_im * tmpl_im
        coef_im = white_im * tmpl_re - white_re * tmpl_im
        widths = ((0, 0), (0, total_len - half_len))
        series = jnp.fft.ifft(lax.complex(jnp.pad(coef_re, widths), jnp.pad(coef_im, widths)), axis=-1) * total_len
        sigma_sq = lax.optimization_barrier(jnp.sum(power * inv_psd, axis=-1))
        magnitude = jnp.abs(series) / jnp.sqrt(sigma_sq)[:, None]
        return magnitude[:, intersection:]
    result = lax.map(one_segment, jnp.arange(SEGMENTS, dtype=jnp.int32))
    return jnp.transpose(result, (1, 0, 2)).reshape(result.shape[1], -1)
```

```python
import functools
import math

import jax
import jax.numpy as jnp
import ml_dtypes
import numpy as np
from jax import lax
from jax.experimental import pallas as pl
from jax.experimental.pallas import tpu as pltpu
from jax.sharding import PartitionSpec as P

N = 1 << 20
K_LOW = N // 200
BF = jnp.bfloat16
F32 = jnp.float32


def halves(x):
    x = np.asarray(x, np.float32)
    hi = x.astype(ml_dtypes.bfloat16)
    lo = (x - hi.astype(np.float32)).astype(ml_dtypes.bfloat16)
    return hi, lo


def unit(num, den, sign):
    ang = (num % den) * (sign * 2.0 * math.pi / den)
    return np.cos(ang), np.sin(ang)


LANE = np.arange(128)
B1 = 64 * (LANE // 64) + 8 * (LANE % 8) + (LANE // 8) % 8


@functools.lru_cache(None)
def tables():
    t = {}
    rows = np.arange(512)
    low = rows // 8 + 64 * (rows % 8)
    c, s = unit(low[:, None] * np.arange(512)[None, :], 512, -1)
    hi, lo = halves(np.concatenate([c, s]))
    t["l1"] = np.stack([hi, lo])
    c, s = unit(low[:, None] * LANE[None, :], 65536, -1)
    t["tw1"] = np.stack([c, s]).astype(np.float32)
    h, al, bh = LANE // 64, (LANE // 8) % 8, LANE % 8
    top = 16 * al + 8 * h + bh
    c, s = unit(LANE[:, None] * top[None, :], 128, -1)
    hi, lo = halves(np.block([[c, s], [-s, c]]))
    t["m2"] = np.concatenate([hi, hi, lo])
    q = low[:, None] + 512 * top[None, :]
    c, s = unit(np.arange(16)[:, None, None] * q[None], N, -1)
    t["tj"] = np.stack([c, s], 1).astype(np.float32)
    a = np.arange(48)
    c, s = unit(a[:, None] * LANE[None, :], 128, 1)
    hi, lo = halves(np.block([[c, s], [-s, c]]))
    t["e1"] = np.concatenate([hi, hi, lo])
    c, s = unit(LANE[:, None] * B1[None, :], 128, 1)
    hi, lo = halves(np.block([[c, -s], [s, c]]))
    t["e2"] = np.concatenate([hi, hi, lo], 1)
    b = 64 * B1[None, :] + np.arange(64)[:, None]
    c, s = unit(b[:, :, None] * LANE[None, None, :], N, 1)
    t["tw"] = np.concatenate([c, s], 1).astype(np.float32)
    c, s = unit(np.arange(64)[:, None] * LANE[None, :], 8192, 1)
    t3 = np.zeros((64, 128, 128), np.float32)
    t3[:, :, 0], t3[:, :, 1] = c, s
    t["tw3"] = t3
    k = np.arange(6)[:, None] * 65536 + np.arange(65536)[None, :]
    amp = np.where(k >= K_LOW, (np.maximum(k, 1) / K_LOW) ** (-7.0 / 6.0), 0.0)
    amp = np.concatenate([amp, np.zeros((2, 65536))])
    t["amp"] = amp.reshape(8, 16, 4096).transpose(1, 0, 2).astype(np.float32)
    return t


def split2(x):
    hi = x.astype(BF)
    lo = (x - hi.astype(F32)).astype(BF)
    return hi, lo


def dot(a, b):
    return jnp.dot(a, b, preferred_element_type=F32)


def psd_kernel(me, bins, vals, amp, g_out, sig_out):
    def tile(i, total):
        at = pl.multiple_of(i * 128, 128)
        idx = bins[:, pl.ds(at, 128)]
        hi, lo = idx >> 7, idx & 127
        acc = jnp.ones((8, 128), F32)
        for h in range(64):
            row = jnp.broadcast_to(vals[h : h + 1, :], (8, 128))
            got = jnp.take_along_axis(row, lo, axis=1)
            acc = jnp.where(hi == h, got, acc)
        inv = 1.0 / acc
        a = amp[0, :, pl.ds(at, 128)]
        g = inv * a
        g_out[:, pl.ds(at, 128)] = g * (1.0 / 1024.0)
        return total + g * a

    total = lax.fori_loop(0, 32, tile, jnp.zeros((8, 128), F32))
    sig_out[...] = jnp.broadcast_to(jnp.sum(total, keepdims=True), (8, 128))


def psd_call(me, bins, vals, amp):
    return pl.pallas_call(
        psd_kernel,
        grid_spec=pltpu.PrefetchScalarGridSpec(
            num_scalar_prefetch=1,
            grid=(1,),
            in_specs=[
                pl.BlockSpec((8, 4096), lambda i, m: (0, 0)),
                pl.BlockSpec((64, 128), lambda i, m: (0, 0)),
                pl.BlockSpec((1, 8, 4096), lambda i, m: (m[0], 0, 0)),
            ],
            out_specs=[
                pl.BlockSpec((8, 4096), lambda i, m: (0, 0)),
                pl.BlockSpec((8, 128), lambda i, m: (0, 0)),
            ],
        ),
        out_shape=[
            jax.ShapeDtypeStruct((8, 4096), F32),
            jax.ShapeDtypeStruct((8, 128), F32),
        ],
    )(me, bins, vals, amp)


def fwd_kernel(me, tail, own, l1, tw1, m2, tj, extra, out):
    th, tl = split2(tail[...])
    oh, ol = split2(own[...])
    xh = jnp.concatenate([th, oh])
    xl = jnp.concatenate([tl, ol])
    y = dot(l1[0], xh) + dot(l1[0], xl) + dot(l1[1], xh)
    yr, yi = y[:512], y[512:]
    c, s = tw1[0], tw1[1]
    yr, yi = yr * c - yi * s, yr * s + yi * c
    rh, rl = split2(yr)
    ih, il = split2(yi)
    f = dot(jnp.concatenate([rh, ih, rl, il, rh, ih], 1), m2[...])
    fr, fi = f[:, :128], f[:, 128:]
    c, s = tj[0, 0], tj[0, 1]
    gr, gi = fr * c - fi * s, fr * s + fi * c
    for d in range(16):
        out[d, 0:32, :] = gr[32 * d : 32 * d + 32]
        out[d, 32:64, :] = gi[32 * d : 32 * d + 32]
        out[d, 64:80, :] = extra[d]


def fwd_call(me, tail, own, l1, tw1, m2, tj, extra):
    def whole(x):
        return pl.BlockSpec(x.shape, lambda i, m, n=x.ndim: (0,) * n)

    return pl.pallas_call(
        fwd_kernel,
        grid_spec=pltpu.PrefetchScalarGridSpec(
            num_scalar_prefetch=1,
            grid=(1,),
            in_specs=[
                whole(tail),
                whole(own),
                whole(l1),
                whole(tw1),
                whole(m2),
                pl.BlockSpec((1, 2, 512, 128), lambda i, m: (m[0], 0, 0, 0)),
                whole(extra),
            ],
            out_specs=pl.BlockSpec((16, 80, 128), lambda i, m: (0, 0, 0)),
        ),
        out_shape=jax.ShapeDtypeStruct((16, 80, 128), F32),
        compiler_params=pltpu.CompilerParams(vmem_limit_bytes=40 << 20),
    )(me, tail, own, l1, tw1, m2, tj, extra)


def swap_groups(x):
    row = lax.broadcasted_iota(jnp.int32, x.shape, 0)
    lane = lax.broadcasted_iota(jnp.int32, x.shape, 1)
    n = x.shape[0]
    for t in range(3):
        d, w = 1 << t, 8 << t
        rb, lb = (row >> t) & 1, (lane >> (3 + t)) & 1
        up = pltpu.roll(pltpu.roll(x, d, 0), 128 - w, 1)
        dn = pltpu.roll(pltpu.roll(x, n - d, 0), w, 1)
        x = jnp.where(rb == lb, x, jnp.where(rb == 1, up, dn))
    return x


def mix_kernel(p, w_out, sig_out):
    lane = lax.broadcasted_iota(jnp.int32, (8, 128), 1)
    for ah in range(6):
        re = jnp.zeros((32, 128), F32)
        im = jnp.zeros((32, 128), F32)
        for j in range(16):
            c = math.cos(2 * math.pi * (j * ah % 16) / 16)
            s = -math.sin(2 * math.pi * (j * ah % 16) / 16)
            pr = p[80 * j : 80 * j + 32, :]
            pi = p[80 * j + 32 : 80 * j + 64, :]
            re = re + (pr * c - pi * s)
            im = im + (pr * s + pi * c)
        re, im = swap_groups(re), swap_groups(im)
        for pair in range(2):
            row = 64 + 2 * ah + pair
            g0 = p[pl.ds(row, 8, stride=160), :]
            g1 = p[pl.ds(row + 80, 8, stride=160), :]
            g = (
                jnp.where(lane < 64, g0, pltpu.roll(g1, 64, 1)),
                jnp.where(lane < 64, pltpu.roll(g0, 64, 1), g1),
            )
            for odd in range(2):
                b = 2 * pair + odd
                w_out[b, 8 * ah : 8 * ah + 8, :] = re[8 * b : 8 * b + 8] * g[odd]
                w_out[b, 48 + 8 * ah : 56 + 8 * ah, :] = im[8 * b : 8 * b + 8] * g[odd]
    sig = jnp.sum(p[pl.ds(76, 16, stride=80), :], axis=0, keepdims=True)
    sig_out[...] = jnp.broadcast_to(lax.rsqrt(sig), (8, 128))


def mix_call(p):
    return pl.pallas_call(
        mix_kernel,
        out_shape=[
            jax.ShapeDtypeStruct((4, 96, 128), F32),
            jax.ShapeDtypeStruct((8, 128), F32),
        ],
    )(p)


def inv_kernel(b0s, w, ph, tw, tw3, e1, e2, *rest):
    h_out = rest[-1]
    wr, wi = w[0, 0:48, :], w[0, 48:96, :]
    zr, zi = [], []
    for m in range(2):
        c, s = ph[m, 0, 0], ph[m, 0, 1]
        v = jnp.concatenate([wr * c - wi * s, wr * s + wi * c])
        vh, vl = split2(v)
        g = lax.dot_general(
            jnp.concatenate([vh, vl, vh]),
            e1[...],
            (((0,), (0,)), ((), ())),
            preferred_element_type=F32,
        )
        gr, gi = g[:, :128], g[:, 128:]
        c, s = tw[0, :128], tw[0, 128:]
        zr.append(gr * c - gi * s)
        zi.append(gr * s + gi * c)
    z = jnp.concatenate([jnp.concatenate(zr, 1), jnp.concatenate(zi, 1)], 0)
    zh, zl = split2(z)
    h = dot(e2[...], jnp.concatenate([zh, zl, zh], 0))
    c, s = tw3[0, :, 0:1], tw3[0, :, 1:2]
    hr, hi = h[:128], h[128:]
    h_out[0, 0] = hr * c - hi * s
    h_out[0, 1] = hr * s + hi * c


def inv_call(b0s, w, ph, tw, tw3, e1, e2, prev):
    count = w.shape[0]
    in_specs = [
        pl.BlockSpec((1, 96, 128), lambda i, b: (i, 0, 0)),
        pl.BlockSpec((2, 1, 2, 48, 128), lambda i, b: (0, b[i], 0, 0, 0)),
        pl.BlockSpec((1, 256, 128), lambda i, b: (b[i], 0, 0)),
        pl.BlockSpec((1, 128, 128), lambda i, b: (b[i], 0, 0)),
        pl.BlockSpec((288, 256), lambda i, b: (0, 0)),
        pl.BlockSpec((256, 768), lambda i, b: (0, 0)),
    ]
    args = [b0s, w, ph, tw, tw3, e1, e2]
    alias = {}
    if prev is not None:
        in_specs.append(pl.BlockSpec(memory_space=pl.ANY))
        args.append(prev)
        alias = {7: 0}
    return pl.pallas_call(
        inv_kernel,
        grid_spec=pltpu.PrefetchScalarGridSpec(
            num_scalar_prefetch=1,
            grid=(count,),
            in_specs=in_specs,
            out_specs=pl.BlockSpec((1, 2, 128, 256), lambda i, b: (b[i], 0, 0, 0)),
        ),
        out_shape=jax.ShapeDtypeStruct((64, 2, 128, 256), F32),
        input_output_aliases=alias,
        compiler_params=pltpu.CompilerParams(vmem_limit_bytes=32 << 20),
        cost_estimate=pl.CostEstimate(
            flops=count * 300_000_000, bytes_accessed=count * 700_000, transcendentals=0
        ),
    )(*args)


def cmul(x, num, den):
    num %= den
    re, im = x
    if num == 0:
        return re, im
    if 4 * num == den:
        return -im, re
    if 2 * num == den:
        return -re, -im
    if 4 * num == 3 * den:
        return im, -re
    c = float(math.cos(2 * math.pi * num / den))
    s = float(math.sin(2 * math.pi * num / den))
    if (8 * num) % den == 0:
        r = math.sqrt(0.5)
        a = r if c > 0 else -r
        b = r if s > 0 else -r
        if a == b:
            return a * (re - im), a * (re + im)
        return a * (re + im), a * (im - re)
    return re * c - im * s, re * s + im * c


def add(x, y):
    return x[0] + y[0], x[1] + y[1]


def sub(x, y):
    return x[0] - y[0], x[1] - y[1]


def fft4(x):
    p, q = add(x[0], x[2]), sub(x[0], x[2])
    r, s = add(x[1], x[3]), sub(x[1], x[3])
    s = (-s[1], s[0])
    return [add(p, r), add(q, s), sub(p, r), sub(q, s)]


def out_kernel(h, sig, out, mid):
    scale = sig[...]
    for m in range(2):
        at = slice(128 * m, 128 * m + 128)
        for lo in range(8):
            x = [(h[8 * hi + lo, 0, :, at], h[8 * hi + lo, 1, :, at]) for hi in range(8)]
            ev, od = fft4(x[0::2]), fft4(x[1::2])
            for f in range(4):
                o = cmul(od[f], f, 8)
                for f2, v in ((f, add(ev[f], o)), (f + 4, sub(ev[f], o))):
                    v = cmul(v, lo * f2, 64)
                    mid[f2, lo, 0] = v[0]
                    mid[f2, lo, 1] = v[1]
        for f2 in range(8):
            x = [(mid[f2, lo, 0], mid[f2, lo, 1]) for lo in range(8)]
            ev, od = fft4(x[0::2]), fft4(x[1::2])
            for f in range(4):
                v = sub(ev[f], cmul(od[f], f, 8))
                mag = jnp.sqrt(v[0] * v[0] + v[1] * v[1]) * scale
                out[f2 + 8 * f, pl.ds(m, 8, stride=2), :] = mag


def out_call(h, sig):
    return pl.pallas_call(
        out_kernel,
        grid=(16,),
        in_specs=[
            pl.BlockSpec((64, 2, 8, 256), lambda i: (0, 0, i, 0)),
            pl.BlockSpec((8, 128), lambda i: (0, 0)),
        ],
        out_specs=pl.BlockSpec((32, 16, 128), lambda i: (0, i, 0)),
        out_shape=jax.ShapeDtypeStruct((32, 256, 128), F32),
        scratch_shapes=[pltpu.VMEM((8, 8, 2, 8, 128), F32)],
        compiler_params=pltpu.CompilerParams(vmem_limit_bytes=32 << 20),
    )(h, sig)


def place(y, x, c):
    return (y % 2 * 4 + x % 4) * 2 + c


def sent(v, dy, dx, dc):
    route = [
        (place(y, x, c), place(y + dy, x + dx, (c + dc) % 2))
        for y in range(2)
        for x in range(4)
        for c in range(2)
    ]
    return lax.ppermute(v, "tmpl", route)


def phases(chirp_slope, chirp_curve):
    s, c = chirp_slope[:, None, None], chirp_curve[:, None, None]
    b0 = jnp.arange(64, dtype=jnp.int32)
    b = 64 * jnp.asarray(B1, jnp.int32)[None, :] + b0[:, None]
    p = (s * b[None] + c * (b * b % N)[None]) % N
    ang = p.astype(F32) * (2 * math.pi / N)
    pc, ps = jnp.cos(ang)[:, :, None, :], jnp.sin(ang)[:, :, None, :]
    a = jnp.arange(48, dtype=jnp.int32)
    p = a[None, None, :] * ((s + 2 * c * b0[None, :, None]) % 128) % 128
    ang = p.astype(F32) * (2 * math.pi / 128)
    qc, qs = jnp.cos(ang)[:, :, :, None], jnp.sin(ang)[:, :, :, None]
    return jnp.stack([pc * qc - ps * qs, pc * qs + ps * qc], 2)


def local(strain, psd_bins, psd_values, chirp_slope, chirp_curve):
    t = {k: jnp.asarray(v) for k, v in tables().items()}
    member = lax.axis_index("tmpl")
    me = member.astype(jnp.int32).reshape(1)
    own = strain.reshape(256, 128)
    count = lax.axis_size("tm")
    tail = lax.ppermute(own, "tm", [(i, i + 1) for i in range(count - 1)])

    g, sig = psd_call(me, psd_bins, psd_values.reshape(64, 128), t["amp"])
    g = g[:6].reshape(6, 8, 8, 16, 4).transpose(3, 0, 4, 2, 1).reshape(16, 12, 128)
    sig = jnp.broadcast_to(sig[0, 0], (16, 4, 128))
    extra = jnp.concatenate([g, sig], 1)

    sent_out = fwd_call(me, tail, own, t["l1"], t["tw1"], t["m2"], t["tj"], extra)
    parts = lax.all_to_all(sent_out, "tmpl", split_axis=0, concat_axis=0, tiled=True)
    w, scale = mix_call(parts.reshape(1280, 128))

    ph = phases(chirp_slope, chirp_curve)
    y, x, c = member // 8, member // 2 % 4, member % 2

    def ids(dy, dx, dc, rows):
        d = ((y + dy) % 2 * 4 + (x + dx) % 4) * 2 + (c + dc) % 2
        return (4 * d + jnp.arange(rows.start, rows.stop)).astype(jnp.int32)

    def work(blocks, prev):
        mine = jnp.concatenate([v for v, *_ in blocks])
        other = sent(mine, 0, 0, 1)
        both = jnp.concatenate([mine, other])
        order = [ids(dy, dx, 0, rows) for _, dy, dx, rows in blocks]
        order += [ids(dy, dx, 1, rows) for _, dy, dx, rows in blocks]
        return inv_call(
            jnp.concatenate(order), both, ph, t["tw"], t["tw3"], t["e1"], t["e2"], prev
        )

    full, first, last = slice(0, 4), slice(0, 2), slice(2, 4)
    up = sent(w, 1, 0, 0)
    right = sent(w, 0, 1, 0)
    left = sent(w, 0, -1, 0)
    h = work([(w, 0, 0, full)], None)
    right2 = sent(jnp.concatenate([up, right[:2]]), 0, 1, 0)
    left2 = sent(jnp.concatenate([up, left[2:]]), 0, -1, 0)
    h = work([(up, 1, 0, full), (right, 0, -1, full), (left, 0, 1, full)], h)
    right3 = sent(right2[:2], 0, 1, 0)
    left3 = sent(left2[2:4], 0, -1, 0)
    h = work(
        [
            (right2[:4], 1, -1, full),
            (left2[:4], 1, 1, full),
            (right2[4:], 0, -2, first),
            (left2[4:], 0, 2, last),
        ],
        h,
    )
    h = work([(right3, 1, -2, first), (left3, 1, 2, last)], h)
    out = out_call(h, scale)
    return out.reshape(4096, 2, 128).transpose(1, 0, 2).reshape(2, 4096 * 128)


def solution(mesh):
    placed = (P("tmpl", "tm"), P(None, "tmpl"), P("tm", None), P("tmpl"), P("tmpl"))
    return jax.shard_map(
        local, mesh=mesh, in_specs=placed, out_specs=P("tmpl", "tm"), check_vma=False
    )
```

```python
import functools
import math

import jax
import jax.numpy as jnp
import ml_dtypes
import numpy as np
from jax import lax
from jax.experimental import pallas as pl
from jax.experimental.pallas import tpu as pltpu
from jax.sharding import PartitionSpec as P

N = 1 << 20
K_LOW = N // 200
BF = jnp.bfloat16
F32 = jnp.float32


def halves(x):
    x = np.asarray(x, np.float32)
    hi = x.astype(ml_dtypes.bfloat16)
    lo = (x - hi.astype(np.float32)).astype(ml_dtypes.bfloat16)
    return hi, lo


def unit(num, den, sign):
    ang = (num % den) * (sign * 2.0 * math.pi / den)
    return np.cos(ang), np.sin(ang)


LANE = np.arange(128)


def bits(x, *order):
    out = 0 * x
    for b in order:
        out = 2 * out + (x >> b & 1)
    return out


B1 = bits(LANE, 2, 1, 6, 5, 4, 3, 0)
SWAP = (0, 3, 4)


@functools.lru_cache(None)
def tables():
    t = {}
    rows = np.arange(512)
    low = rows // 8 + 64 * (rows % 8)
    c, s = unit(low[:, None] * np.arange(512)[None, :], 512, -1)
    hi, lo = halves(np.concatenate([c, s]))
    t["l1"] = np.stack([hi, lo])
    c, s = unit(low[:, None] * LANE[None, :], 65536, -1)
    t["tw1"] = np.stack([c, s]).astype(np.float32)
    top = 16 * bits(LANE, 4, 3, 0) + (B1 >> 3)
    c, s = unit(LANE[:, None] * top[None, :], 128, -1)
    hi, lo = halves(np.block([[c, s], [-s, c]]))
    t["m2"] = np.concatenate([hi, hi, lo])
    q = low[:, None] + 512 * top[None, :]
    c, s = unit(np.arange(16)[:, None, None] * q[None], N, -1)
    t["tj"] = np.stack([c, s], 1).astype(np.float32)
    a = np.arange(48)
    c, s = unit(a[:, None] * LANE[None, :], 128, 1)
    hi, lo = halves(np.block([[c, s], [-s, c]]))
    t["e1"] = np.concatenate([hi, hi, lo])
    c, s = unit(LANE[:, None] * B1[None, :], 128, 1)
    hi, lo = halves(np.block([[c, -s], [s, c]]))
    t["e2"] = np.concatenate([hi, hi, lo], 1)
    b = 64 * B1[None, :] + np.arange(64)[:, None]
    c, s = unit(b[:, :, None] * LANE[None, None, :], N, 1)
    t["tw"] = np.concatenate([c, s], 1).astype(np.float32)
    c, s = unit(np.arange(64)[:, None] * LANE[None, :], 8192, 1)
    t3 = np.zeros((64, 128, 128), np.float32)
    t3[:, :, 0], t3[:, :, 1] = c, s
    t["tw3"] = t3
    k = np.arange(6)[:, None] * 65536 + np.arange(65536)[None, :]
    amp = np.where(k >= K_LOW, (np.maximum(k, 1) / K_LOW) ** (-7.0 / 6.0), 0.0)
    amp = np.concatenate([amp, np.zeros((2, 65536))])
    t["amp"] = amp.reshape(8, 16, 4096).transpose(1, 0, 2).astype(np.float32)
    return t


def split2(x):
    hi = x.astype(BF)
    lo = (x - hi.astype(F32)).astype(BF)
    return hi, lo


def dot(a, b):
    return jnp.dot(a, b, preferred_element_type=F32)


def psd_kernel(me, bins, vals, amp, out, g):
    width = 512

    def tile(i, total):
        at = pl.multiple_of(i * width, width)
        idx = bins[:, pl.ds(at, width)]
        parts = [idx[:, 128 * q : 128 * q + 128] for q in range(width // 128)]
        hi, lo = [v >> 7 for v in parts], [v & 127 for v in parts]
        acc = [jnp.ones((8, 128), F32) for _ in parts]
        for h in range(64):
            row = jnp.broadcast_to(vals[h : h + 1, :], (8, 128))
            for q in range(len(parts)):
                got = jnp.take_along_axis(row, lo[q], axis=1)
                acc[q] = jnp.where(hi[q] == h, got, acc[q])
        for q in range(len(parts)):
            pos = pl.multiple_of(at + 128 * q, 128)
            a = amp[0, :, pl.ds(pos, 128)]
            f = a / acc[q]
            total = total + f * a
            row8 = pl.multiple_of(i * (width // 16) + 8 * q, 8)
            g[pl.ds(row8, 8), :] = f * (1.0 / 1024.0)
        return total

    total = lax.fori_loop(0, 4096 // width, tile, jnp.zeros((8, 128), F32))
    share = jnp.broadcast_to(jnp.sum(total, keepdims=True), (256, 128))
    row = lax.broadcasted_iota(jnp.int32, (256, 128), 0) & 7
    full = jnp.where(row >= 6, share, g[...])
    for half in range(2):
        tr = full[128 * half : 128 * half + 128].T
        for low in range(2):
            for d in range(16):
                at = 8 * half + 4 * low
                out[d, at : at + 4, :] = tr[64 * low + 4 * d : 64 * low + 4 * d + 4]


def psd_call(me, bins, vals, amp):
    return pl.pallas_call(
        psd_kernel,
        grid_spec=pltpu.PrefetchScalarGridSpec(
            num_scalar_prefetch=1,
            grid=(1,),
            in_specs=[
                pl.BlockSpec((8, 4096), lambda i, m: (0, 0)),
                pl.BlockSpec((64, 128), lambda i, m: (0, 0)),
                pl.BlockSpec((1, 8, 4096), lambda i, m: (m[0], 0, 0)),
            ],
            out_specs=pl.BlockSpec((16, 16, 128), lambda i, m: (0, 0, 0)),
            scratch_shapes=[pltpu.VMEM((256, 128), F32)],
        ),
        out_shape=jax.ShapeDtypeStruct((16, 16, 128), F32),
        compiler_params=pltpu.CompilerParams(vmem_limit_bytes=50 << 20),
    )(me, bins, vals, amp)


def fwd_kernel(me, tail, own, l1, tw1, m2, tj, extra, out):
    th, tl = split2(tail[...])
    oh, ol = split2(own[...])
    xh = jnp.concatenate([th, oh])
    xl = jnp.concatenate([tl, ol])
    y = dot(l1[0], xh) + dot(l1[0], xl) + dot(l1[1], xh)
    yr, yi = y[:512], y[512:]
    c, s = tw1[0], tw1[1]
    yr, yi = yr * c - yi * s, yr * s + yi * c
    rh, rl = split2(yr)
    ih, il = split2(yi)
    f = dot(jnp.concatenate([rh, ih, rl, il, rh, ih], 1), m2[...])
    fr, fi = f[:, :128], f[:, 128:]
    c, s = tj[0, 0], tj[0, 1]
    gr, gi = fr * c - fi * s, fr * s + fi * c
    for d in range(16):
        out[d, 0:32, :] = gr[32 * d : 32 * d + 32]
        out[d, 32:64, :] = gi[32 * d : 32 * d + 32]
        out[d, 64:80, :] = extra[d]


def fwd_call(me, tail, own, l1, tw1, m2, tj, extra):
    def whole(x):
        return pl.BlockSpec(x.shape, lambda i, m, n=x.ndim: (0,) * n)

    return pl.pallas_call(
        fwd_kernel,
        grid_spec=pltpu.PrefetchScalarGridSpec(
            num_scalar_prefetch=1,
            grid=(1,),
            in_specs=[
                whole(tail),
                whole(own),
                whole(l1),
                whole(tw1),
                whole(m2),
                pl.BlockSpec((1, 2, 512, 128), lambda i, m: (m[0], 0, 0, 0)),
                whole(extra),
            ],
            out_specs=pl.BlockSpec((16, 80, 128), lambda i, m: (0, 0, 0)),
        ),
        out_shape=jax.ShapeDtypeStruct((16, 80, 128), F32),
        compiler_params=pltpu.CompilerParams(vmem_limit_bytes=50 << 20),
    )(me, tail, own, l1, tw1, m2, tj, extra)


def swap_groups(x):
    row = lax.broadcasted_iota(jnp.int32, x.shape, 0)
    lane = lax.broadcasted_iota(jnp.int32, x.shape, 1)
    n = x.shape[0]
    for t in range(3):
        d, w = 1 << t, 1 << SWAP[t]
        rb, lb = (row >> t) & 1, (lane >> SWAP[t]) & 1
        up = pltpu.roll(pltpu.roll(x, d, 0), 128 - w, 1)
        dn = pltpu.roll(pltpu.roll(x, n - d, 0), w, 1)
        x = jnp.where(rb == lb, x, jnp.where(rb == 1, up, dn))
    return x


def swap_low_bits(v):
    lane = lax.broadcasted_iota(jnp.int32, v[0].shape, 1)
    v = list(v)
    for t in range(3):
        w = 1 << t
        clear = (lane >> t) & 1 == 0
        for i in range(8):
            if not i & w:
                p, q = v[i], v[i | w]
                v[i] = jnp.where(clear, p, pltpu.roll(q, w, 1))
                v[i | w] = jnp.where(clear, pltpu.roll(p, 128 - w, 1), q)
    return v


def mix_kernel(p, w_out, sig_out):
    g = []
    for b in range(4):
        rows = [64 + 80 * (i >> 2) + 4 * (i & 3) + b for i in range(8)]
        g.append(swap_low_bits([p[pl.ds(r, 8, stride=160), :] for r in rows]))
    for ah in range(6):
        re = jnp.zeros((32, 128), F32)
        im = jnp.zeros((32, 128), F32)
        for j in range(16):
            c = math.cos(2 * math.pi * (j * ah % 16) / 16)
            s = -math.sin(2 * math.pi * (j * ah % 16) / 16)
            pr = p[80 * j : 80 * j + 32, :]
            pi = p[80 * j + 32 : 80 * j + 64, :]
            re = re + (pr * c - pi * s)
            im = im + (pr * s + pi * c)
        re, im = swap_groups(re), swap_groups(im)
        for b in range(4):
            at = slice(8 * b, 8 * b + 8)
            w_out[b, 8 * ah : 8 * ah + 8, :] = re[at] * g[b][ah]
            w_out[b, 48 + 8 * ah : 56 + 8 * ah, :] = im[at] * g[b][ah]
    sig = jnp.sum(g[0][6], keepdims=True) * (1.0 / 64.0)
    sig_out[...] = jnp.broadcast_to(lax.rsqrt(sig), (8, 128))


def mix_call(p):
    return pl.pallas_call(
        mix_kernel,
        out_shape=[
            jax.ShapeDtypeStruct((4, 96, 128), F32),
            jax.ShapeDtypeStruct((8, 128), F32),
        ],
    )(p)


def inv_kernel(me, w, phc, phs, tw, tw3, e1, e2, *rest):
    h_out = rest[-1]
    core = me[0] & 1
    for u in range(8):
        at = (u // 4 ^ core) * 4 + u % 4
        wr, wi = w[0, at, 0:48, :], w[0, at, 48:96, :]
        v = []
        for m in range(2):
            c, s = phc[m, u], phs[m, u]
            v.append(jnp.concatenate([wr * c - wi * s, wr * s + wi * c]))
        vh, vl = split2(jnp.concatenate(v, 1))
        g = lax.dot_general(
            jnp.concatenate([vh, vl, vh]),
            e1[...],
            (((0,), (0,)), ((), ())),
            preferred_element_type=F32,
        )
        c, s = tw[u, :128], tw[u, 128:]
        zr, zi = [], []
        for m in range(2):
            gr, gi = g[128 * m : 128 * m + 128, :128], g[128 * m : 128 * m + 128, 128:]
            zr.append(gr * c - gi * s)
            zi.append(gr * s + gi * c)
        z = jnp.concatenate([jnp.concatenate(zr, 1), jnp.concatenate(zi, 1)], 0)
        zh, zl = split2(z)
        h = dot(e2[...], jnp.concatenate([zh, zl, zh], 0))
        c, s = tw3[u, :, 0:1], tw3[u, :, 1:2]
        hr, hi = h[:128], h[128:]
        h_out[u, 0] = hr * c - hi * s
        h_out[u, 1] = hr * s + hi * c


def inv_call(me, w, chips, ph, tw, tw3, e1, e2, prev):
    count = len(chips)

    def chip(i, m):
        y, x = m[0] >> 3, (m[0] >> 1) & 3
        dy, dx = chips[0]
        for n in range(1, count):
            dy = jnp.where(i == n, chips[n][0], dy)
            dx = jnp.where(i == n, chips[n][1], dx)
        return ((y + dy) & 1) * 4 + ((x + dx) & 3)

    in_specs = [
        pl.BlockSpec((1, 8, 96, 128), lambda i, m: (i, 0, 0, 0)),
        pl.BlockSpec((2, 8, 48, 128), lambda i, m: (0, chip(i, m), 0, 0)),
        pl.BlockSpec((2, 8, 48, 128), lambda i, m: (0, chip(i, m), 0, 0)),
        pl.BlockSpec((8, 256, 128), lambda i, m: (chip(i, m), 0, 0)),
        pl.BlockSpec((8, 128, 128), lambda i, m: (chip(i, m), 0, 0)),
        pl.BlockSpec((288, 256), lambda i, m: (0, 0)),
        pl.BlockSpec((256, 768), lambda i, m: (0, 0)),
    ]
    args = [me, w, *ph, tw, tw3, e1, e2]
    alias = {}
    if prev is not None:
        in_specs.append(pl.BlockSpec(memory_space=pl.ANY))
        args.append(prev)
        alias = {8: 0}
    return pl.pallas_call(
        inv_kernel,
        grid_spec=pltpu.PrefetchScalarGridSpec(
            num_scalar_prefetch=1,
            grid=(count,),
            in_specs=in_specs,
            out_specs=pl.BlockSpec((8, 2, 128, 256), lambda i, m: (chip(i, m), 0, 0, 0)),
        ),
        out_shape=jax.ShapeDtypeStruct((64, 2, 128, 256), F32),
        input_output_aliases=alias,
        compiler_params=pltpu.CompilerParams(vmem_limit_bytes=50 << 20),
        cost_estimate=pl.CostEstimate(
            flops=count * 1_500_000_000, bytes_accessed=count * 6_000_000, transcendentals=0
        ),
    )(*args)


def cmul(x, num, den):
    num %= den
    re, im = x
    if num == 0:
        return re, im
    if 4 * num == den:
        return -im, re
    if 2 * num == den:
        return -re, -im
    if 4 * num == 3 * den:
        return im, -re
    c = float(math.cos(2 * math.pi * num / den))
    s = float(math.sin(2 * math.pi * num / den))
    if (8 * num) % den == 0:
        r = math.sqrt(0.5)
        a = r if c > 0 else -r
        b = r if s > 0 else -r
        if a == b:
            return a * (re - im), a * (re + im)
        return a * (re + im), a * (im - re)
    return re * c - im * s, re * s + im * c


def add(x, y):
    return x[0] + y[0], x[1] + y[1]


def sub(x, y):
    return x[0] - y[0], x[1] - y[1]


def fft4(x):
    p, q = add(x[0], x[2]), sub(x[0], x[2])
    r, s = add(x[1], x[3]), sub(x[1], x[3])
    s = (-s[1], s[0])
    return [add(p, r), add(q, s), sub(p, r), sub(q, s)]


def out_kernel(h, sig, out, mid):
    scale = sig[...]
    for m in range(2):
        at = slice(128 * m, 128 * m + 128)
        for lo in range(8):
            x = [(h[8 * hi + lo, 0, :, at], h[8 * hi + lo, 1, :, at]) for hi in range(8)]
            ev, od = fft4(x[0::2]), fft4(x[1::2])
            for f in range(4):
                o = cmul(od[f], f, 8)
                for f2, v in ((f, add(ev[f], o)), (f + 4, sub(ev[f], o))):
                    v = cmul(v, lo * f2, 64)
                    mid[f2, lo, 0] = v[0]
                    mid[f2, lo, 1] = v[1]
        for f2 in range(8):
            x = [(mid[f2, lo, 0], mid[f2, lo, 1]) for lo in range(8)]
            ev, od = fft4(x[0::2]), fft4(x[1::2])
            for f in range(4):
                v = sub(ev[f], cmul(od[f], f, 8))
                power = v[0] * v[0] + v[1] * v[1]
                mag = power * lax.rsqrt(jnp.maximum(power, 1e-37)) * scale
                out[f2 + 8 * f, pl.ds(m, 8, stride=2), :] = mag


def out_call(h, sig):
    return pl.pallas_call(
        out_kernel,
        grid=(16,),
        in_specs=[
            pl.BlockSpec((64, 2, 8, 256), lambda i: (0, 0, i, 0)),
            pl.BlockSpec((8, 128), lambda i: (0, 0)),
        ],
        out_specs=pl.BlockSpec((32, 16, 128), lambda i: (0, i, 0)),
        out_shape=jax.ShapeDtypeStruct((32, 256, 128), F32),
        scratch_shapes=[pltpu.VMEM((8, 8, 2, 8, 128), F32)],
        compiler_params=pltpu.CompilerParams(vmem_limit_bytes=58 << 20),
    )(h, sig)


def place(y, x, c):
    return (y % 2 * 4 + x % 4) * 2 + c


def sent(v, dy, dx, dc):
    route = [
        (place(y, x, c), place(y + dy, x + dx, (c + dc) % 2))
        for y in range(2)
        for x in range(4)
        for c in range(2)
    ]
    return lax.ppermute(v, "tmpl", route)


def phases(chirp_slope, chirp_curve):
    s, c = chirp_slope[:, None, None], chirp_curve[:, None, None]
    b0 = jnp.arange(64, dtype=jnp.int32)
    b = 64 * jnp.asarray(B1, jnp.int32)[None, :] + b0[:, None]
    p = (s * b[None] + c * (b * b % N)[None]) % N
    ang = p.astype(F32) * (2 * math.pi / N)
    pc, ps = jnp.cos(ang)[:, :, None, :], jnp.sin(ang)[:, :, None, :]
    a = jnp.arange(48, dtype=jnp.int32)
    p = a[None, None, :] * ((s + 2 * c * b0[None, :, None]) % 128) % 128
    ang = p.astype(F32) * (2 * math.pi / 128)
    qc, qs = jnp.cos(ang)[:, :, :, None], jnp.sin(ang)[:, :, :, None]
    return pc * qc - ps * qs, pc * qs + ps * qc


def local(strain, psd_bins, psd_values, chirp_slope, chirp_curve):
    t = {k: jnp.asarray(v) for k, v in tables().items()}
    member = lax.axis_index("tmpl")
    me = member.astype(jnp.int32).reshape(1)
    own = strain.reshape(256, 128)
    count = lax.axis_size("tm")
    tail = lax.ppermute(own, "tm", [(i, i + 1) for i in range(count - 1)])

    extra = psd_call(me, psd_bins, psd_values.reshape(64, 128), t["amp"])
    sent_out = fwd_call(me, tail, own, t["l1"], t["tw1"], t["m2"], t["tj"], extra)
    sent_out, chirp_slope, chirp_curve = lax.optimization_barrier(
        (sent_out, chirp_slope, chirp_curve)
    )
    parts = lax.all_to_all(sent_out, "tmpl", split_axis=0, concat_axis=0, tiled=True)
    ph = phases(chirp_slope, chirp_curve)
    w, scale = mix_call(parts.reshape(1280, 128))

    def work(blocks, chips, prev):
        mine = jnp.stack(blocks)
        both = jnp.concatenate([mine, sent(mine, 0, 0, 1)], 1)
        return inv_call(me, both, chips, ph, t["tw"], t["tw3"], t["e1"], t["e2"], prev)

    up = sent(w, 1, 0, 0)
    right = sent(w, 0, 1, 0)
    left = sent(w, 0, -1, 0)
    h = work([w], [(0, 0)], None)
    right2 = sent(jnp.concatenate([up, right[:2]]), 0, 1, 0)
    left2 = sent(jnp.concatenate([up, left[2:]]), 0, -1, 0)
    h = work([up, right, left], [(1, 0), (0, -1), (0, 1)], h)
    right2, left2, h = lax.optimization_barrier((right2, left2, h))
    right3 = sent(right2[:2], 0, 1, 0)
    left3 = sent(left2[2:4], 0, -1, 0)
    far = jnp.concatenate([right2[4:], left2[4:]])
    h = work([right2[:4], left2[:4], far], [(1, -1), (1, 1), (0, 2)], h)
    h = work([jnp.concatenate([right3, left3])], [(1, 2)], h)
    out = out_call(h, scale)
    return out.reshape(4096, 2, 128).transpose(1, 0, 2).reshape(2, 4096 * 128)


def solution(mesh):
    placed = (P("tmpl", "tm"), P(None, "tmpl"), P("tm", None), P("tmpl"), P("tmpl"))
    return jax.shard_map(
        local, mesh=mesh, in_specs=placed, out_specs=P("tmpl", "tm"), check_vma=False
    )
```

```python
import functools
import math

import jax
import jax.numpy as jnp
import ml_dtypes
import numpy as np
from jax import lax
from jax.experimental import pallas as pl
from jax.experimental.pallas import tpu as pltpu
from jax.sharding import PartitionSpec as P

N = 1 << 20
K_LOW = N // 200
BF = jnp.bfloat16
F32 = jnp.float32
INV_VMEM = 24 << 20
OUT_VMEM = 24 << 20


def halves(x):
    x = np.asarray(x, np.float32)
    hi = x.astype(ml_dtypes.bfloat16)
    lo = (x - hi.astype(np.float32)).astype(ml_dtypes.bfloat16)
    return hi, lo


def unit(num, den, sign):
    ang = (num % den) * (sign * 2.0 * math.pi / den)
    return np.cos(ang), np.sin(ang)


LANE = np.arange(128)


def bits(x, *order):
    out = 0 * x
    for b in order:
        out = 2 * out + (x >> b & 1)
    return out


B1 = bits(LANE, 2, 1, 6, 5, 4, 3, 0)
SWAP = (0, 3, 4)


@functools.lru_cache(None)
def tables():
    t = {}
    rows = np.arange(512)
    low = rows // 8 + 64 * (rows % 8)
    c, s = unit(low[:, None] * np.arange(512)[None, :], 512, -1)
    hi, lo = halves(np.concatenate([c, s]))
    t["l1"] = np.stack([hi, lo])
    c, s = unit(low[:, None] * LANE[None, :], 65536, -1)
    t["tw1"] = np.stack([c, s]).astype(np.float32)
    top = 16 * bits(LANE, 4, 3, 0) + (B1 >> 3)
    c, s = unit(LANE[:, None] * top[None, :], 128, -1)
    hi, lo = halves(np.block([[c, s], [-s, c]]))
    t["m2"] = np.concatenate([hi, hi, lo])
    q = low[:, None] + 512 * top[None, :]
    c, s = unit(np.arange(16)[:, None, None] * q[None], N, -1)
    t["tj"] = np.stack([c, s], 1).astype(np.float32)
    a = np.arange(48)
    c, s = unit(a[:, None] * LANE[None, :], 128, 1)
    hi, lo = halves(np.block([[c, s], [-s, c]]))
    t["e1"] = np.concatenate([hi, hi, lo])
    c, s = unit(LANE[:, None] * B1[None, :], 128, 1)
    hi, lo = halves(np.block([[c, -s], [s, c]]))
    t["e2"] = np.concatenate([hi, hi, lo], 1)
    c, s = unit(64 * B1[:, None] * LANE[None, :], N, 1)
    t["tw"] = np.stack([c, s]).astype(np.float32)
    c, s = unit(np.arange(64)[:, None] * LANE[None, :], N, 1)
    t["twb"] = np.stack([c, s], 1).astype(np.float32)
    c, s = unit(np.arange(64)[:, None] * LANE[None, :], 8192, 1)
    t3 = np.zeros((8, 128, 128), np.float32)
    t3[:, :, 0:8] = c.reshape(8, 8, 128).transpose(0, 2, 1)
    t3[:, :, 8:16] = s.reshape(8, 8, 128).transpose(0, 2, 1)
    t["tw3"] = t3
    k = np.arange(6)[:, None] * 65536 + np.arange(65536)[None, :]
    amp = np.where(k >= K_LOW, (np.maximum(k, 1) / K_LOW) ** (-7.0 / 6.0), 0.0)
    amp = np.concatenate([amp, np.zeros((2, 65536))])
    t["amp"] = amp.reshape(8, 16, 4096).transpose(1, 0, 2).astype(np.float32)
    return t


def split2(x):
    hi = x.astype(BF)
    lo = (x - hi.astype(F32)).astype(BF)
    return hi, lo


def dot(a, b):
    return jnp.dot(a, b, preferred_element_type=F32)


def psd_kernel(me, bins, vals, amp, out, g):
    width = 512

    def tile(i, total):
        at = pl.multiple_of(i * width, width)
        idx = bins[:, pl.ds(at, width)]
        parts = [idx[:, 128 * q : 128 * q + 128] for q in range(width // 128)]
        hi, lo = [v >> 7 for v in parts], [v & 127 for v in parts]
        acc = [jnp.ones((8, 128), F32) for _ in parts]
        for h in range(64):
            row = jnp.broadcast_to(vals[h : h + 1, :], (8, 128))
            for q in range(len(parts)):
                got = jnp.take_along_axis(row, lo[q], axis=1)
                acc[q] = jnp.where(hi[q] == h, got, acc[q])
        for q in range(len(parts)):
            pos = pl.multiple_of(at + 128 * q, 128)
            a = amp[0, :, pl.ds(pos, 128)]
            f = a / acc[q]
            total = total + f * a
            row8 = pl.multiple_of(i * (width // 16) + 8 * q, 8)
            g[pl.ds(row8, 8), :] = f * (1.0 / 1024.0)
        return total

    total = lax.fori_loop(0, 4096 // width, tile, jnp.zeros((8, 128), F32))
    share = jnp.broadcast_to(jnp.sum(total, keepdims=True), (256, 128))
    row = lax.broadcasted_iota(jnp.int32, (256, 128), 0) & 7
    full = jnp.where(row >= 6, share, g[...])
    for half in range(2):
        tr = full[128 * half : 128 * half + 128].T
        for low in range(2):
            for d in range(16):
                at = 8 * half + 4 * low
                out[d, at : at + 4, :] = tr[64 * low + 4 * d : 64 * low + 4 * d + 4]


def psd_call(me, bins, vals, amp):
    return pl.pallas_call(
        psd_kernel,
        grid_spec=pltpu.PrefetchScalarGridSpec(
            num_scalar_prefetch=1,
            grid=(1,),
            in_specs=[
                pl.BlockSpec((8, 4096), lambda i, m: (0, 0)),
                pl.BlockSpec((64, 128), lambda i, m: (0, 0)),
                pl.BlockSpec((1, 8, 4096), lambda i, m: (m[0], 0, 0)),
            ],
            out_specs=pl.BlockSpec((16, 16, 128), lambda i, m: (0, 0, 0)),
            scratch_shapes=[pltpu.VMEM((256, 128), F32)],
        ),
        out_shape=jax.ShapeDtypeStruct((16, 16, 128), F32),
        compiler_params=pltpu.CompilerParams(vmem_limit_bytes=50 << 20),
    )(me, bins, vals, amp)


def fwd_kernel(me, tail, own, l1, tw1, m2, tj, extra, out):
    th, tl = split2(tail[...])
    oh, ol = split2(own[...])
    xh = jnp.concatenate([th, oh])
    xl = jnp.concatenate([tl, ol])
    y = dot(l1[0], xh) + dot(l1[0], xl) + dot(l1[1], xh)
    yr, yi = y[:512], y[512:]
    c, s = tw1[0], tw1[1]
    yr, yi = yr * c - yi * s, yr * s + yi * c
    rh, rl = split2(yr)
    ih, il = split2(yi)
    f = dot(jnp.concatenate([rh, ih, rl, il, rh, ih], 1), m2[...])
    fr, fi = f[:, :128], f[:, 128:]
    c, s = tj[0, 0], tj[0, 1]
    gr, gi = fr * c - fi * s, fr * s + fi * c
    for d in range(16):
        out[d, 0:32, :] = gr[32 * d : 32 * d + 32]
        out[d, 32:64, :] = gi[32 * d : 32 * d + 32]
        out[d, 64:80, :] = extra[d]


def fwd_call(me, tail, own, l1, tw1, m2, tj, extra):
    def whole(x):
        return pl.BlockSpec(x.shape, lambda i, m, n=x.ndim: (0,) * n)

    return pl.pallas_call(
        fwd_kernel,
        grid_spec=pltpu.PrefetchScalarGridSpec(
            num_scalar_prefetch=1,
            grid=(1,),
            in_specs=[
                whole(tail),
                whole(own),
                whole(l1),
                whole(tw1),
                whole(m2),
                pl.BlockSpec((1, 2, 512, 128), lambda i, m: (m[0], 0, 0, 0)),
                whole(extra),
            ],
            out_specs=pl.BlockSpec((16, 80, 128), lambda i, m: (0, 0, 0)),
        ),
        out_shape=jax.ShapeDtypeStruct((16, 80, 128), F32),
        compiler_params=pltpu.CompilerParams(vmem_limit_bytes=50 << 20),
    )(me, tail, own, l1, tw1, m2, tj, extra)


def swap_groups(x):
    row = lax.broadcasted_iota(jnp.int32, x.shape, 0)
    lane = lax.broadcasted_iota(jnp.int32, x.shape, 1)
    n = x.shape[0]
    for t in range(3):
        d, w = 1 << t, 1 << SWAP[t]
        rb, lb = (row >> t) & 1, (lane >> SWAP[t]) & 1
        up = pltpu.roll(pltpu.roll(x, d, 0), 128 - w, 1)
        dn = pltpu.roll(pltpu.roll(x, n - d, 0), w, 1)
        x = jnp.where(rb == lb, x, jnp.where(rb == 1, up, dn))
    return x


def swap_low_bits(v):
    lane = lax.broadcasted_iota(jnp.int32, v[0].shape, 1)
    v = list(v)
    for t in range(3):
        w = 1 << t
        clear = (lane >> t) & 1 == 0
        for i in range(8):
            if not i & w:
                p, q = v[i], v[i | w]
                v[i] = jnp.where(clear, p, pltpu.roll(q, w, 1))
                v[i | w] = jnp.where(clear, pltpu.roll(p, 128 - w, 1), q)
    return v


def mix_kernel(p, w_out, sig_out):
    g = []
    for b in range(4):
        rows = [64 + 80 * (i >> 2) + 4 * (i & 3) + b for i in range(8)]
        g.append(swap_low_bits([p[pl.ds(r, 8, stride=160), :] for r in rows]))
    for ah in range(6):
        re = jnp.zeros((32, 128), F32)
        im = jnp.zeros((32, 128), F32)
        for j in range(16):
            c = math.cos(2 * math.pi * (j * ah % 16) / 16)
            s = -math.sin(2 * math.pi * (j * ah % 16) / 16)
            pr = p[80 * j : 80 * j + 32, :]
            pi = p[80 * j + 32 : 80 * j + 64, :]
            re = re + (pr * c - pi * s)
            im = im + (pr * s + pi * c)
        re, im = swap_groups(re), swap_groups(im)
        for b in range(4):
            at = slice(8 * b, 8 * b + 8)
            w_out[b, 8 * ah : 8 * ah + 8, :] = re[at] * g[b][ah]
            w_out[b, 48 + 8 * ah : 56 + 8 * ah, :] = im[at] * g[b][ah]
    sig = jnp.sum(g[0][6], keepdims=True) * (1.0 / 64.0)
    sig_out[...] = jnp.broadcast_to(lax.rsqrt(sig), (8, 128))


def mix_call(p):
    return pl.pallas_call(
        mix_kernel,
        out_shape=[
            jax.ShapeDtypeStruct((4, 96, 128), F32),
            jax.ShapeDtypeStruct((8, 128), F32),
        ],
    )(p)


def inv_kernel(me, w, phi, psi, tw, twb, tw3, e1, e2, *rest):
    h_out = rest[-1]
    core = me[0] & 1
    for u in range(8):
        at = (u // 4 ^ core) * 4 + u % 4
        wr, wi = w[0, at, 0:48, :], w[0, at, 48:96, :]
        v = []
        for m in range(2):
            pc, ps = phi[0, u, 2 * m : 2 * m + 1, :], phi[0, u, 2 * m + 1 : 2 * m + 2, :]
            lane = 16 * m + u
            qc, qs = psi[0, :, lane : lane + 1], psi[0, :, lane + 8 : lane + 9]
            c, s = pc * qc - ps * qs, pc * qs + ps * qc
            v.append(jnp.concatenate([wr * c - wi * s, wr * s + wi * c]))
        vh, vl = split2(jnp.concatenate(v, 1))
        g = lax.dot_general(
            jnp.concatenate([vh, vl, vh]),
            e1[...],
            (((0,), (0,)), ((), ())),
            preferred_element_type=F32,
        )
        fc, fs, bc, bs = tw[0], tw[1], twb[u, 0:1, :], twb[u, 1:2, :]
        c, s = fc * bc - fs * bs, fc * bs + fs * bc
        zr, zi = [], []
        for m in range(2):
            gr, gi = g[128 * m : 128 * m + 128, :128], g[128 * m : 128 * m + 128, 128:]
            zr.append(gr * c - gi * s)
            zi.append(gr * s + gi * c)
        z = jnp.concatenate([jnp.concatenate(zr, 1), jnp.concatenate(zi, 1)], 0)
        zh, zl = split2(z)
        h = dot(e2[...], jnp.concatenate([zh, zl, zh], 0))
        c, s = tw3[0, :, u : u + 1], tw3[0, :, u + 8 : u + 9]
        hr, hi = h[:128], h[128:]
        h_out[:, u, 0] = (hr * c - hi * s).reshape(16, 8, 256)
        h_out[:, u, 1] = (hr * s + hi * c).reshape(16, 8, 256)


def inv_call(me, w, chips, ph, t, prev):
    count = len(chips)

    def chip(i, m):
        y, x = m[0] >> 3, (m[0] >> 1) & 3
        dy, dx = chips[0]
        for n in range(1, count):
            dy = jnp.where(i == n, chips[n][0], dy)
            dx = jnp.where(i == n, chips[n][1], dx)
        return ((y + dy) & 1) * 4 + ((x + dx) & 3)

    in_specs = [
        pl.BlockSpec((1, 8, 96, 128), lambda i, m: (i, 0, 0, 0)),
        pl.BlockSpec((1, 8, 4, 128), lambda i, m: (chip(i, m), 0, 0, 0)),
        pl.BlockSpec((1, 48, 128), lambda i, m: (chip(i, m), 0, 0)),
        pl.BlockSpec((2, 128, 128), lambda i, m: (0, 0, 0)),
        pl.BlockSpec((8, 2, 128), lambda i, m: (chip(i, m), 0, 0)),
        pl.BlockSpec((1, 128, 128), lambda i, m: (chip(i, m), 0, 0)),
        pl.BlockSpec((288, 256), lambda i, m: (0, 0)),
        pl.BlockSpec((256, 768), lambda i, m: (0, 0)),
    ]
    args = [me, w, *ph, t["tw"], t["twb"], t["tw3"], t["e1"], t["e2"]]
    alias = {}
    if prev is not None:
        in_specs.append(pl.BlockSpec(memory_space=pl.ANY))
        args.append(prev)
        alias = {9: 0}
    return pl.pallas_call(
        inv_kernel,
        grid_spec=pltpu.PrefetchScalarGridSpec(
            num_scalar_prefetch=1,
            grid=(count,),
            in_specs=in_specs,
            out_specs=pl.BlockSpec(
                (16, 8, 2, 8, 256), lambda i, m: (0, chip(i, m), 0, 0, 0)
            ),
        ),
        out_shape=jax.ShapeDtypeStruct((16, 64, 2, 8, 256), F32),
        input_output_aliases=alias,
        compiler_params=pltpu.CompilerParams(vmem_limit_bytes=INV_VMEM),
        cost_estimate=pl.CostEstimate(
            flops=count * 1_500_000_000, bytes_accessed=count * 3_000_000, transcendentals=0
        ),
    )(*args)


def cmul(x, num, den):
    num %= den
    re, im = x
    if num == 0:
        return re, im
    if 4 * num == den:
        return -im, re
    if 2 * num == den:
        return -re, -im
    if 4 * num == 3 * den:
        return im, -re
    c = float(math.cos(2 * math.pi * num / den))
    s = float(math.sin(2 * math.pi * num / den))
    if (8 * num) % den == 0:
        r = math.sqrt(0.5)
        a = r if c > 0 else -r
        b = r if s > 0 else -r
        if a == b:
            return a * (re - im), a * (re + im)
        return a * (re + im), a * (im - re)
    return re * c - im * s, re * s + im * c


def add(x, y):
    return x[0] + y[0], x[1] + y[1]


def sub(x, y):
    return x[0] - y[0], x[1] - y[1]


def fft4(x):
    p, q = add(x[0], x[2]), sub(x[0], x[2])
    r, s = add(x[1], x[3]), sub(x[1], x[3])
    s = (-s[1], s[0])
    return [add(p, r), add(q, s), sub(p, r), sub(q, s)]


def out_kernel(h, sig, out, mid):
    scale = sig[...]
    for m in range(2):
        at = slice(128 * m, 128 * m + 128)
        for lo in range(8):
            x = [(h[0, 8 * hi + lo, 0, :, at], h[0, 8 * hi + lo, 1, :, at]) for hi in range(8)]
            ev, od = fft4(x[0::2]), fft4(x[1::2])
            for f in range(4):
                o = cmul(od[f], f, 8)
                for f2, v in ((f, add(ev[f], o)), (f + 4, sub(ev[f], o))):
                    v = cmul(v, lo * f2, 64)
                    mid[f2, lo, 0] = v[0]
                    mid[f2, lo, 1] = v[1]
        for f2 in range(8):
            x = [(mid[f2, lo, 0], mid[f2, lo, 1]) for lo in range(8)]
            ev, od = fft4(x[0::2]), fft4(x[1::2])
            for f in range(4):
                v = sub(ev[f], cmul(od[f], f, 8))
                power = v[0] * v[0] + v[1] * v[1]
                mag = power * lax.rsqrt(jnp.maximum(power, 1e-37)) * scale
                out[f2 + 8 * f, pl.ds(m, 8, stride=2), :] = mag


def out_call(h, sig):
    return pl.pallas_call(
        out_kernel,
        grid=(16,),
        in_specs=[
            pl.BlockSpec((1, 64, 2, 8, 256), lambda i: (i, 0, 0, 0, 0)),
            pl.BlockSpec((8, 128), lambda i: (0, 0)),
        ],
        out_specs=pl.BlockSpec((32, 16, 128), lambda i: (0, i, 0)),
        out_shape=jax.ShapeDtypeStruct((32, 256, 128), F32),
        scratch_shapes=[pltpu.VMEM((8, 8, 2, 8, 128), F32)],
        compiler_params=pltpu.CompilerParams(vmem_limit_bytes=OUT_VMEM),
    )(h, sig)


def place(y, x, c):
    return (y % 2 * 4 + x % 4) * 2 + c


def sent(v, dy, dx, dc):
    route = [
        (place(y, x, c), place(y + dy, x + dx, (c + dc) % 2))
        for y in range(2)
        for x in range(4)
        for c in range(2)
    ]
    return lax.ppermute(v, "tmpl", route)


def phases(chirp_slope, chirp_curve):
    row = jnp.arange(4, dtype=jnp.int32)[None, :, None]
    s = jnp.where(row < 2, chirp_slope[0], chirp_slope[1])
    c = jnp.where(row < 2, chirp_curve[0], chirp_curve[1])
    b0 = jnp.arange(64, dtype=jnp.int32)[:, None, None]
    b = 64 * jnp.asarray(B1, jnp.int32)[None, None, :] + b0
    p = (s * b + c * (b * b % N) - (N // 4) * (row % 2)) % N
    phi = jnp.cos(p.astype(F32) * (2 * math.pi / N))
    lane = jnp.arange(128, dtype=jnp.int32)[None, None, :]
    s = jnp.where(lane < 16, chirp_slope[0], chirp_slope[1])
    c = jnp.where(lane < 16, chirp_curve[0], chirp_curve[1])
    b0 = 8 * jnp.arange(8, dtype=jnp.int32)[:, None, None] + lane % 8
    a = jnp.arange(48, dtype=jnp.int32)[None, :, None]
    p = (a * ((s + 2 * c * b0) % 128) - 32 * (lane // 8 % 2)) % 128
    psi = jnp.cos(p.astype(F32) * (2 * math.pi / 128))
    return phi.reshape(8, 8, 4, 128), psi


def local(strain, psd_bins, psd_values, chirp_slope, chirp_curve):
    t = {k: jnp.asarray(v) for k, v in tables().items()}
    member = lax.axis_index("tmpl")
    me = member.astype(jnp.int32).reshape(1)
    own = strain.reshape(256, 128)
    count = lax.axis_size("tm")
    tail = lax.ppermute(own, "tm", [(i, i + 1) for i in range(count - 1)])

    extra = psd_call(me, psd_bins, psd_values.reshape(64, 128), t["amp"])
    sent_out = fwd_call(me, tail, own, t["l1"], t["tw1"], t["m2"], t["tj"], extra)
    sent_out, chirp_slope, chirp_curve = lax.optimization_barrier(
        (sent_out, chirp_slope, chirp_curve)
    )
    parts = lax.all_to_all(sent_out, "tmpl", split_axis=0, concat_axis=0, tiled=True)
    ph = phases(chirp_slope, chirp_curve)
    parts, *ph = lax.optimization_barrier((parts, *ph))
    w, scale = mix_call(parts.reshape(1280, 128))

    def work(blocks, chips, prev):
        mine = jnp.stack(blocks)
        both = jnp.concatenate([mine, sent(mine, 0, 0, 1)], 1)
        return inv_call(me, both, chips, ph, t, prev)

    up = sent(w, 1, 0, 0)
    right = sent(w, 0, 1, 0)
    left = sent(w, 0, -1, 0)
    h = work([w], [(0, 0)], None)
    right2 = sent(jnp.concatenate([up, right[:2]]), 0, 1, 0)
    left2 = sent(jnp.concatenate([up, left[2:]]), 0, -1, 0)
    h = work([up, right, left], [(1, 0), (0, -1), (0, 1)], h)
    right2, left2, h = lax.optimization_barrier((right2, left2, h))
    right3 = sent(right2[:2], 0, 1, 0)
    left3 = sent(left2[2:4], 0, -1, 0)
    far = jnp.concatenate([right2[4:], left2[4:]])
    h = work([right2[:4], left2[:4], far], [(1, -1), (1, 1), (0, 2)], h)
    h = work([jnp.concatenate([right3, left3])], [(1, 2)], h)
    out = out_call(h, scale)
    return out.reshape(4096, 2, 128).transpose(1, 0, 2).reshape(2, 4096 * 128)


def solution(mesh):
    placed = (P("tmpl", "tm"), P(None, "tmpl"), P("tm", None), P("tmpl"), P("tmpl"))
    return jax.shard_map(
        local, mesh=mesh, in_specs=placed, out_specs=P("tmpl", "tm"), check_vma=False
    )
```

```python
import functools
import math

import jax
import jax.numpy as jnp
import ml_dtypes
import numpy as np
from jax import lax
from jax.experimental import pallas as pl
from jax.experimental.pallas import tpu as pltpu
from jax.sharding import PartitionSpec as P

N = 1 << 20
K_LOW = N // 200
BF = jnp.bfloat16
F32 = jnp.float32
INV_VMEM = 24 << 20
FWD_VMEM = 58 << 20
OUT_VMEM = 24 << 20


def halves(x):
    x = np.asarray(x, np.float32)
    hi = x.astype(ml_dtypes.bfloat16)
    lo = (x - hi.astype(np.float32)).astype(ml_dtypes.bfloat16)
    return hi, lo


def unit(num, den, sign):
    ang = (num % den) * (sign * 2.0 * math.pi / den)
    return np.cos(ang), np.sin(ang)


LANE = np.arange(128)


def bits(x, *order):
    out = 0 * x
    for b in order:
        out = 2 * out + (x >> b & 1)
    return out


B1 = bits(LANE, 2, 1, 6, 5, 4, 3, 0)
SWAP = (0, 3, 4)


@functools.lru_cache(None)
def tables():
    t = {}
    rows = np.arange(512)
    low = rows // 8 + 64 * (rows % 8)
    c, s = unit(low[:, None] * np.arange(512)[None, :], 512, -1)
    hi, lo = halves(np.concatenate([c, s]))
    t["l1"] = np.stack([hi, lo])
    c, s = unit(low[:, None] * LANE[None, :], 65536, -1)
    t["tw1"] = np.stack([c, s]).astype(np.float32)
    top = 16 * bits(LANE, 4, 3, 0) + (B1 >> 3)
    c, s = unit(LANE[:, None] * top[None, :], 128, -1)
    hi, lo = halves(np.block([[c, s], [-s, c]]))
    t["m2"] = np.concatenate([hi, hi, lo])
    q = low[:, None] + 512 * top[None, :]
    c, s = unit(np.arange(16)[:, None, None] * q[None], N, -1)
    t["tj"] = np.stack([c, s], 1).astype(np.float32)
    a = np.arange(48)
    c, s = unit(a[:, None] * LANE[None, :], 128, 1)
    hi, lo = halves(np.block([[c, s], [-s, c]]))
    t["e1"] = np.concatenate([hi, hi, lo])
    c, s = unit(LANE[:, None] * B1[None, :], 128, 1)
    hi, lo = halves(np.block([[c, -s], [s, c]]))
    t["e2"] = np.concatenate([hi, hi, lo], 1)
    c, s = unit(64 * B1[:, None] * LANE[None, :], N, 1)
    t["tw"] = np.stack([c, s]).astype(np.float32)
    c, s = unit(np.arange(64)[:, None] * LANE[None, :], N, 1)
    t["twb"] = np.stack([c, s], 1).astype(np.float32)
    c, s = unit(np.arange(64)[:, None] * LANE[None, :], 8192, 1)
    t3 = np.zeros((8, 128, 128), np.float32)
    t3[:, :, 0:8] = c.reshape(8, 8, 128).transpose(0, 2, 1)
    t3[:, :, 8:16] = s.reshape(8, 8, 128).transpose(0, 2, 1)
    t["tw3"] = t3
    return t


def split2(x):
    hi = x.astype(BF)
    lo = (x - hi.astype(F32)).astype(BF)
    return hi, lo


def dot(a, b):
    return jnp.dot(a, b, preferred_element_type=F32)


def psd_kernel(me, bins_hbm, vals_hbm, out, g, tr, bins, vals, sems):
    fetch = [
        pltpu.make_async_copy(bins_hbm, bins, sems.at[0]),
        pltpu.make_async_copy(vals_hbm, vals, sems.at[1]),
    ]
    for copy in fetch:
        copy.start()
    row = lax.broadcasted_iota(jnp.int32, (256, 128), 0)
    lane = lax.broadcasted_iota(jnp.int32, (256, 128), 1)
    k = (row & 7) * 65536 + me[0] * 4096 + (row >> 3) * 128 + lane
    ratio = jnp.maximum(k.astype(F32) / K_LOW, 1.0)
    amp = jnp.where(k >= K_LOW, jnp.exp(jnp.log(ratio) * (-7.0 / 6.0)), 0.0)
    for copy in fetch:
        copy.wait()
    v0 = vals[...]
    p0 = v0.astype(BF)
    v1 = v0 - p0.astype(F32)
    p1 = v1.astype(BF)
    p2 = (v1 - p1.astype(F32)).astype(BF)
    parts = jnp.concatenate([p0, p1, p2])
    width = 512
    low = lax.broadcasted_iota(jnp.int32, (128, width), 0)
    high = lax.broadcasted_iota(jnp.int32, (64, width), 0)
    g[...] = jnp.ones((256, 128), F32)

    def chunk(i, carry):
        at = pl.multiple_of(i * width, width)
        idx = bins[:, pl.ds(at, width)]
        for ah in range(6):
            one = idx[ah : ah + 1]
            hot = jnp.where((one & 127) == low, 1.0, 0.0).astype(BF)
            got = dot(parts, hot)
            got = got[:64] + got[64:128] + got[128:]
            got = jnp.sum(jnp.where((one >> 7) == high, got, 0.0), axis=0, keepdims=True)
            for q in range(width // 128):
                g[pl.ds(i * (width // 16) + 8 * q + ah, 1), :] = got[:, 128 * q : 128 * q + 128]
        return carry

    lax.fori_loop(0, 4096 // width, chunk, 0)
    f = amp / g[...]
    rows = (row & 7) < 6
    share = jnp.sum(jnp.where(rows, f * amp, 0.0), keepdims=True)
    full = jnp.where(rows, f * (1.0 / 1024.0), jnp.broadcast_to(share, (256, 128)))
    for half in range(2):
        tr[...] = full[128 * half : 128 * half + 128].T
        for low_bit in range(2):
            for d in range(16):
                at = 8 * half + 4 * low_bit
                src = 64 * low_bit + 4 * d
                out[d, at : at + 4, :] = tr[src : src + 4, :]


def psd_call(me, bins, vals):
    return pl.pallas_call(
        psd_kernel,
        grid_spec=pltpu.PrefetchScalarGridSpec(
            num_scalar_prefetch=1,
            grid=(1,),
            in_specs=[pl.BlockSpec(memory_space=pl.ANY)] * 2,
            out_specs=pl.BlockSpec((16, 16, 128), lambda i, m: (0, 0, 0)),
            scratch_shapes=[
                pltpu.VMEM((256, 128), F32),
                pltpu.VMEM((128, 128), F32),
                pltpu.VMEM((8, 4096), jnp.int32),
                pltpu.VMEM((64, 128), F32),
                pltpu.SemaphoreType.DMA((2,)),
            ],
        ),
        out_shape=jax.ShapeDtypeStruct((16, 16, 128), F32),
        compiler_params=pltpu.CompilerParams(vmem_limit_bytes=16 << 20),
    )(me, bins, vals)


def fwd_kernel(me, tail, own, l1, tw1, m2, tj, extra, out):
    th, tl = split2(tail[...])
    oh, ol = split2(own[...])
    xh = jnp.concatenate([th, oh])
    xl = jnp.concatenate([tl, ol])
    y = dot(l1[0], xh) + dot(l1[0], xl) + dot(l1[1], xh)
    yr, yi = y[:512], y[512:]
    c, s = tw1[0], tw1[1]
    yr, yi = yr * c - yi * s, yr * s + yi * c
    rh, rl = split2(yr)
    ih, il = split2(yi)
    f = dot(jnp.concatenate([rh, ih, rl, il, rh, ih], 1), m2[...])
    fr, fi = f[:, :128], f[:, 128:]
    c, s = tj[0, 0], tj[0, 1]
    gr, gi = fr * c - fi * s, fr * s + fi * c
    for d in range(16):
        out[d, 0:32, :] = gr[32 * d : 32 * d + 32]
        out[d, 32:64, :] = gi[32 * d : 32 * d + 32]
        out[d, 64:80, :] = extra[d]


def fwd_call(me, tail, own, l1, tw1, m2, tj, extra):
    def whole(x):
        return pl.BlockSpec(x.shape, lambda i, m, n=x.ndim: (0,) * n)

    return pl.pallas_call(
        fwd_kernel,
        grid_spec=pltpu.PrefetchScalarGridSpec(
            num_scalar_prefetch=1,
            grid=(1,),
            in_specs=[
                whole(tail),
                whole(own),
                whole(l1),
                whole(tw1),
                whole(m2),
                pl.BlockSpec((1, 2, 512, 128), lambda i, m: (m[0], 0, 0, 0)),
                whole(extra),
            ],
            out_specs=pl.BlockSpec((16, 80, 128), lambda i, m: (0, 0, 0)),
        ),
        out_shape=jax.ShapeDtypeStruct((16, 80, 128), F32),
        compiler_params=pltpu.CompilerParams(vmem_limit_bytes=FWD_VMEM),
    )(me, tail, own, l1, tw1, m2, tj, extra)


def swap_groups(x):
    row = lax.broadcasted_iota(jnp.int32, x.shape, 0)
    lane = lax.broadcasted_iota(jnp.int32, x.shape, 1)
    n = x.shape[0]
    for t in range(3):
        d, w = 1 << t, 1 << SWAP[t]
        rb, lb = (row >> t) & 1, (lane >> SWAP[t]) & 1
        up = pltpu.roll(pltpu.roll(x, d, 0), 128 - w, 1)
        dn = pltpu.roll(pltpu.roll(x, n - d, 0), w, 1)
        x = jnp.where(rb == lb, x, jnp.where(rb == 1, up, dn))
    return x


def swap_low_bits(v):
    lane = lax.broadcasted_iota(jnp.int32, v[0].shape, 1)
    v = list(v)
    for t in range(3):
        w = 1 << t
        clear = (lane >> t) & 1 == 0
        for i in range(8):
            if not i & w:
                p, q = v[i], v[i | w]
                v[i] = jnp.where(clear, p, pltpu.roll(q, w, 1))
                v[i | w] = jnp.where(clear, pltpu.roll(p, 128 - w, 1), q)
    return v


def mix_kernel(p, w_out, sig_out):
    g = []
    for b in range(4):
        rows = [64 + 80 * (i >> 2) + 4 * (i & 3) + b for i in range(8)]
        g.append(swap_low_bits([p[pl.ds(r, 8, stride=160), :] for r in rows]))
    quarters = []
    for n in range(4):
        rows = [80 * (n + 4 * q) for q in range(4)]
        quarters.append(fft4([(p[i + 32 : i + 64, :], p[i : i + 32, :]) for i in rows]))
    for ah in range(6):
        z = [cmul(quarters[n][ah % 4], n * ah, 16) for n in range(4)]
        im, re = add(add(z[0], z[1]), add(z[2], z[3]))
        re, im = swap_groups(re), swap_groups(im)
        for b in range(4):
            at = slice(8 * b, 8 * b + 8)
            w_out[b, 8 * ah : 8 * ah + 8, :] = re[at] * g[b][ah]
            w_out[b, 48 + 8 * ah : 56 + 8 * ah, :] = im[at] * g[b][ah]
    sig = jnp.sum(g[0][6], keepdims=True) * (1.0 / 64.0)
    sig_out[...] = jnp.broadcast_to(lax.rsqrt(sig), (8, 128))


def mix_call(p):
    return pl.pallas_call(
        mix_kernel,
        out_shape=[
            jax.ShapeDtypeStruct((4, 96, 128), F32),
            jax.ShapeDtypeStruct((8, 128), F32),
        ],
        compiler_params=pltpu.CompilerParams(vmem_limit_bytes=16 << 20),
    )(p)


def inv_kernel(me, w, phi, psi, tw, twb, tw3, e1, e2, *rest):
    h_out = rest[-1]
    core = me[0] & 1
    for u in range(8):
        at = (u // 4 ^ core) * 4 + u % 4
        wr, wi = w[0, at, 0:48, :], w[0, at, 48:96, :]
        v = []
        for m in range(2):
            pc, ps = phi[0, u, 2 * m : 2 * m + 1, :], phi[0, u, 2 * m + 1 : 2 * m + 2, :]
            lane = 16 * m + u
            qc, qs = psi[0, :, lane : lane + 1], psi[0, :, lane + 8 : lane + 9]
            c, s = pc * qc - ps * qs, pc * qs + ps * qc
            v.append(jnp.concatenate([wr * c - wi * s, wr * s + wi * c]))
        vh, vl = split2(jnp.concatenate(v, 1))
        g = lax.dot_general(
            jnp.concatenate([vh, vl, vh]),
            e1[...],
            (((0,), (0,)), ((), ())),
            preferred_element_type=F32,
        )
        fc, fs, bc, bs = tw[0], tw[1], twb[u, 0:1, :], twb[u, 1:2, :]
        c, s = fc * bc - fs * bs, fc * bs + fs * bc
        zr, zi = [], []
        for m in range(2):
            gr, gi = g[128 * m : 128 * m + 128, :128], g[128 * m : 128 * m + 128, 128:]
            zr.append(gr * c - gi * s)
            zi.append(gr * s + gi * c)
        z = jnp.concatenate([jnp.concatenate(zr, 1), jnp.concatenate(zi, 1)], 0)
        zh, zl = split2(z)
        h = dot(e2[...], jnp.concatenate([zh, zl, zh], 0))
        c, s = tw3[0, :, u : u + 1], tw3[0, :, u + 8 : u + 9]
        hr, hi = h[:128], h[128:]
        h_out[:, u, 0] = (hr * c - hi * s).reshape(16, 8, 256)
        h_out[:, u, 1] = (hr * s + hi * c).reshape(16, 8, 256)


def inv_call(me, w, chips, ph, t, prev):
    count = len(chips)

    def chip(i, m):
        y, x = m[0] >> 3, (m[0] >> 1) & 3
        dy, dx = chips[0]
        for n in range(1, count):
            dy = jnp.where(i == n, chips[n][0], dy)
            dx = jnp.where(i == n, chips[n][1], dx)
        return ((y + dy) & 1) * 4 + ((x + dx) & 3)

    in_specs = [
        pl.BlockSpec((1, 8, 96, 128), lambda i, m: (i, 0, 0, 0)),
        pl.BlockSpec((1, 8, 4, 128), lambda i, m: (chip(i, m), 0, 0, 0)),
        pl.BlockSpec((1, 48, 128), lambda i, m: (chip(i, m), 0, 0)),
        pl.BlockSpec((2, 128, 128), lambda i, m: (0, 0, 0)),
        pl.BlockSpec((8, 2, 128), lambda i, m: (chip(i, m), 0, 0)),
        pl.BlockSpec((1, 128, 128), lambda i, m: (chip(i, m), 0, 0)),
        pl.BlockSpec((288, 256), lambda i, m: (0, 0)),
        pl.BlockSpec((256, 768), lambda i, m: (0, 0)),
    ]
    args = [me, w, *ph, t["tw"], t["twb"], t["tw3"], t["e1"], t["e2"]]
    alias = {}
    if prev is not None:
        in_specs.append(pl.BlockSpec(memory_space=pl.ANY))
        args.append(prev)
        alias = {9: 0}
    return pl.pallas_call(
        inv_kernel,
        grid_spec=pltpu.PrefetchScalarGridSpec(
            num_scalar_prefetch=1,
            grid=(count,),
            in_specs=in_specs,
            out_specs=pl.BlockSpec(
                (16, 8, 2, 8, 256), lambda i, m: (0, chip(i, m), 0, 0, 0)
            ),
        ),
        out_shape=jax.ShapeDtypeStruct((16, 64, 2, 8, 256), F32),
        input_output_aliases=alias,
        compiler_params=pltpu.CompilerParams(vmem_limit_bytes=INV_VMEM),
        cost_estimate=pl.CostEstimate(
            flops=count * 1_500_000_000, bytes_accessed=count * 3_000_000, transcendentals=0
        ),
    )(*args)


def cmul(x, num, den):
    num %= den
    re, im = x
    if num == 0:
        return re, im
    if 4 * num == den:
        return -im, re
    if 2 * num == den:
        return -re, -im
    if 4 * num == 3 * den:
        return im, -re
    c = float(math.cos(2 * math.pi * num / den))
    s = float(math.sin(2 * math.pi * num / den))
    if (8 * num) % den == 0:
        r = math.sqrt(0.5)
        a = r if c > 0 else -r
        b = r if s > 0 else -r
        if a == b:
            return a * (re - im), a * (re + im)
        return a * (re + im), a * (im - re)
    return re * c - im * s, re * s + im * c


def add(x, y):
    return x[0] + y[0], x[1] + y[1]


def sub(x, y):
    return x[0] - y[0], x[1] - y[1]


def fft4(x):
    p, q = add(x[0], x[2]), sub(x[0], x[2])
    r, s = add(x[1], x[3]), sub(x[1], x[3])
    s = (-s[1], s[0])
    return [add(p, r), add(q, s), sub(p, r), sub(q, s)]


def out_kernel(h, sig, out, mid):
    scale = sig[...]
    for m in range(2):
        at = slice(128 * m, 128 * m + 128)
        for lo in range(8):
            x = [(h[0, 8 * hi + lo, 0, :, at], h[0, 8 * hi + lo, 1, :, at]) for hi in range(8)]
            ev, od = fft4(x[0::2]), fft4(x[1::2])
            for f in range(4):
                o = cmul(od[f], f, 8)
                for f2, v in ((f, add(ev[f], o)), (f + 4, sub(ev[f], o))):
                    v = cmul(v, lo * f2, 64)
                    mid[f2, lo, 0] = v[0]
                    mid[f2, lo, 1] = v[1]
        for f2 in range(8):
            x = [(mid[f2, lo, 0], mid[f2, lo, 1]) for lo in range(8)]
            ev, od = fft4(x[0::2]), fft4(x[1::2])
            for f in range(4):
                v = sub(ev[f], cmul(od[f], f, 8))
                power = v[0] * v[0] + v[1] * v[1]
                mag = power * lax.rsqrt(jnp.maximum(power, 1e-37)) * scale
                out[f2 + 8 * f, pl.ds(m, 8, stride=2), :] = mag


def out_call(h, sig):
    return pl.pallas_call(
        out_kernel,
        grid=(16,),
        in_specs=[
            pl.BlockSpec((1, 64, 2, 8, 256), lambda i: (i, 0, 0, 0, 0)),
            pl.BlockSpec((8, 128), lambda i: (0, 0)),
        ],
        out_specs=pl.BlockSpec((32, 16, 128), lambda i: (0, i, 0)),
        out_shape=jax.ShapeDtypeStruct((32, 256, 128), F32),
        scratch_shapes=[pltpu.VMEM((8, 8, 2, 8, 128), F32)],
        compiler_params=pltpu.CompilerParams(vmem_limit_bytes=OUT_VMEM),
    )(h, sig)


def place(y, x, c):
    return (y % 2 * 4 + x % 4) * 2 + c


def sent(v, dy, dx, dc):
    route = [
        (place(y, x, c), place(y + dy, x + dx, (c + dc) % 2))
        for y in range(2)
        for x in range(4)
        for c in range(2)
    ]
    return lax.ppermute(v, "tmpl", route)


def phases(chirp_slope, chirp_curve):
    row = jnp.arange(4, dtype=jnp.int32)[None, :, None]
    s = jnp.where(row < 2, chirp_slope[0], chirp_slope[1])
    c = jnp.where(row < 2, chirp_curve[0], chirp_curve[1])
    b0 = jnp.arange(64, dtype=jnp.int32)[:, None, None]
    b = 64 * jnp.asarray(B1, jnp.int32)[None, None, :] + b0
    p = (s * b + c * (b * b % N) - (N // 4) * (row % 2)) % N
    phi = jnp.cos(p.astype(F32) * (2 * math.pi / N))
    lane = jnp.arange(128, dtype=jnp.int32)[None, None, :]
    s = jnp.where(lane < 16, chirp_slope[0], chirp_slope[1])
    c = jnp.where(lane < 16, chirp_curve[0], chirp_curve[1])
    b0 = 8 * jnp.arange(8, dtype=jnp.int32)[:, None, None] + lane % 8
    a = jnp.arange(48, dtype=jnp.int32)[None, :, None]
    p = (a * ((s + 2 * c * b0) % 128) - 32 * (lane // 8 % 2)) % 128
    psi = jnp.cos(p.astype(F32) * (2 * math.pi / 128))
    return phi.reshape(8, 8, 4, 128), psi


def local(strain, psd_bins, psd_values, chirp_slope, chirp_curve):
    t = {k: jnp.asarray(v) for k, v in tables().items()}
    member = lax.axis_index("tmpl")
    me = member.astype(jnp.int32).reshape(1)
    own = strain.reshape(256, 128)
    count = lax.axis_size("tm")
    tail = lax.ppermute(own, "tm", [(i, i + 1) for i in range(count - 1)])

    extra = psd_call(me, psd_bins, psd_values.reshape(64, 128))
    sent_out = fwd_call(me, tail, own, t["l1"], t["tw1"], t["m2"], t["tj"], extra)
    sent_out, chirp_slope, chirp_curve = lax.optimization_barrier(
        (sent_out, chirp_slope, chirp_curve)
    )
    parts = lax.all_to_all(sent_out, "tmpl", split_axis=0, concat_axis=0, tiled=True)
    ph = phases(chirp_slope, chirp_curve)
    parts, *ph = lax.optimization_barrier((parts, *ph))
    w, scale = mix_call(parts.reshape(1280, 128))

    def work(blocks, chips, prev):
        mine = jnp.stack(blocks)
        both = jnp.concatenate([mine, sent(mine, 0, 0, 1)], 1)
        return inv_call(me, both, chips, ph, t, prev)

    up = sent(w, 1, 0, 0)
    right = sent(w, 0, 1, 0)
    left = sent(w, 0, -1, 0)
    h = work([w], [(0, 0)], None)
    up, right, left, h = lax.optimization_barrier((up, right, left, h))
    right2 = sent(jnp.concatenate([up, right[:2]]), 0, 1, 0)
    left2 = sent(jnp.concatenate([up, left[2:]]), 0, -1, 0)
    h = work([up, right, left], [(1, 0), (0, -1), (0, 1)], h)
    right2, left2, h = lax.optimization_barrier((right2, left2, h))
    right3 = sent(right2[:2], 0, 1, 0)
    left3 = sent(left2[2:4], 0, -1, 0)
    far = jnp.concatenate([right2[4:], left2[4:]])
    h = work([right2[:4], left2[:4], far], [(1, -1), (1, 1), (0, 2)], h)
    right3, left3, h = lax.optimization_barrier((right3, left3, h))
    h = work([jnp.concatenate([right3, left3])], [(1, 2)], h)
    out = out_call(h, scale)
    return out.reshape(4096, 2, 128).transpose(1, 0, 2).reshape(2, 4096 * 128)


def solution(mesh):
    placed = (P("tmpl", "tm"), P(None, "tmpl"), P("tm", None), P("tmpl"), P("tmpl"))
    return jax.shard_map(
        local, mesh=mesh, in_specs=placed, out_specs=P("tmpl", "tm"), check_vma=False
    )
```

```python
import functools
import math

import jax
import jax.numpy as jnp
import ml_dtypes
import numpy as np
from jax import lax
from jax.experimental import pallas as pl
from jax.experimental.pallas import tpu as pltpu
from jax.sharding import PartitionSpec as P

N = 1 << 20
K_LOW = N // 200
BF = jnp.bfloat16
F32 = jnp.float32
INV_VMEM = 24 << 20
FWD_VMEM = 58 << 20
OUT_VMEM = 24 << 20


def halves(x):
    x = np.asarray(x, np.float32)
    hi = x.astype(ml_dtypes.bfloat16)
    lo = (x - hi.astype(np.float32)).astype(ml_dtypes.bfloat16)
    return hi, lo


def unit(num, den, sign):
    ang = (num % den) * (sign * 2.0 * math.pi / den)
    return np.cos(ang), np.sin(ang)


LANE = np.arange(128)


def bits(x, *order):
    out = 0 * x
    for b in order:
        out = 2 * out + (x >> b & 1)
    return out


B1 = bits(LANE, 2, 1, 6, 5, 4, 3, 0)
SWAP = (0, 3, 4)


@functools.lru_cache(None)
def tables():
    t = {}
    rows = np.arange(512)
    low = rows // 8 + 64 * (rows % 8)
    c, s = unit(low[:, None] * np.arange(512)[None, :], 512, -1)
    hi, lo = halves(np.concatenate([c, s]))
    t["l1"] = np.stack([hi, lo])
    c, s = unit(low[:, None] * LANE[None, :], 65536, -1)
    t["tw1"] = np.stack([c, s]).astype(np.float32)
    top = 16 * bits(LANE, 4, 3, 0) + (B1 >> 3)
    c, s = unit(LANE[:, None] * top[None, :], 128, -1)
    hi, lo = halves(np.block([[c, s], [-s, c]]))
    t["m2"] = np.concatenate([hi, hi, lo])
    q = low[:, None] + 512 * top[None, :]
    c, s = unit(np.arange(16)[:, None, None] * q[None], N, -1)
    t["tj"] = np.stack([c, s], 1).astype(np.float32)
    a = np.arange(48)
    c, s = unit(a[:, None] * LANE[None, :], 128, 1)
    hi, lo = halves(np.block([[c, s], [-s, c]]))
    t["e1"] = np.concatenate([hi, hi, lo])
    c, s = unit(LANE[:, None] * B1[None, :], 128, 1)
    hi, lo = halves(np.block([[c, -s], [s, c]]))
    t["e2"] = np.concatenate([hi, hi, lo], 1)
    c, s = unit(64 * B1[:, None] * LANE[None, :], N, 1)
    t["tw"] = np.stack([c, s]).astype(np.float32)
    c, s = unit(np.arange(64)[:, None] * LANE[None, :], N, 1)
    t["twb"] = np.stack([c, s], 1).astype(np.float32)
    c, s = unit(np.arange(64)[:, None] * LANE[None, :], 8192, 1)
    t3 = np.zeros((8, 128, 128), np.float32)
    t3[:, :, 0:8] = c.reshape(8, 8, 128).transpose(0, 2, 1)
    t3[:, :, 8:16] = s.reshape(8, 8, 128).transpose(0, 2, 1)
    t["tw3"] = t3
    return t


def split2(x):
    hi = x.astype(BF)
    lo = (x - hi.astype(F32)).astype(BF)
    return hi, lo


def dot(a, b):
    return jnp.dot(a, b, preferred_element_type=F32)


def psd_kernel(me, bins_hbm, vals_hbm, out, g, tr, bins, vals, sems):
    fetch = [
        pltpu.make_async_copy(bins_hbm, bins, sems.at[0]),
        pltpu.make_async_copy(vals_hbm, vals, sems.at[1]),
    ]
    for copy in fetch:
        copy.start()
    row = lax.broadcasted_iota(jnp.int32, (256, 128), 0)
    lane = lax.broadcasted_iota(jnp.int32, (256, 128), 1)
    k = (row & 7) * 65536 + me[0] * 4096 + (row >> 3) * 128 + lane
    ratio = jnp.maximum(k.astype(F32) / K_LOW, 1.0)
    amp = jnp.where(k >= K_LOW, jnp.exp(jnp.log(ratio) * (-7.0 / 6.0)), 0.0)
    for copy in fetch:
        copy.wait()
    v0 = vals[...]
    p0 = v0.astype(BF)
    v1 = v0 - p0.astype(F32)
    p1 = v1.astype(BF)
    p2 = (v1 - p1.astype(F32)).astype(BF)
    parts = jnp.concatenate([p0, p1, p2])
    width = 512
    low = lax.broadcasted_iota(jnp.int32, (128, width), 0)
    high = lax.broadcasted_iota(jnp.int32, (64, width), 0)
    g[...] = jnp.ones((256, 128), F32)

    def chunk(i, carry):
        at = pl.multiple_of(i * width, width)
        idx = bins[:, pl.ds(at, width)]
        for ah in range(6):
            one = idx[ah : ah + 1]
            hot = jnp.where((one & 127) == low, 1.0, 0.0).astype(BF)
            got = dot(parts, hot)
            got = got[:64] + got[64:128] + got[128:]
            got = jnp.sum(jnp.where((one >> 7) == high, got, 0.0), axis=0, keepdims=True)
            for q in range(width // 128):
                g[pl.ds(i * (width // 16) + 8 * q + ah, 1), :] = got[:, 128 * q : 128 * q + 128]
        return carry

    lax.fori_loop(0, 4096 // width, chunk, 0)
    f = amp / g[...]
    rows = (row & 7) < 6
    share = jnp.sum(jnp.where(rows, f * amp, 0.0), keepdims=True)
    full = jnp.where(rows, f * (1.0 / 1024.0), jnp.broadcast_to(share, (256, 128)))
    for half in range(2):
        tr[...] = full[128 * half : 128 * half + 128].T
        for low_bit in range(2):
            for d in range(16):
                at = 8 * half + 4 * low_bit
                src = 64 * low_bit + 4 * d
                out[d, at : at + 4, :] = tr[src : src + 4, :]


def psd_call(me, bins, vals):
    return pl.pallas_call(
        psd_kernel,
        grid_spec=pltpu.PrefetchScalarGridSpec(
            num_scalar_prefetch=1,
            grid=(1,),
            in_specs=[pl.BlockSpec(memory_space=pl.ANY)] * 2,
            out_specs=pl.BlockSpec((16, 16, 128), lambda i, m: (0, 0, 0)),
            scratch_shapes=[
                pltpu.VMEM((256, 128), F32),
                pltpu.VMEM((128, 128), F32),
                pltpu.VMEM((8, 4096), jnp.int32),
                pltpu.VMEM((64, 128), F32),
                pltpu.SemaphoreType.DMA((2,)),
            ],
        ),
        out_shape=jax.ShapeDtypeStruct((16, 16, 128), F32),
        compiler_params=pltpu.CompilerParams(vmem_limit_bytes=16 << 20),
    )(me, bins, vals)


def fwd_kernel(me, tail, own, l1, tw1, m2, tj, extra, out):
    th, tl = split2(tail[...])
    oh, ol = split2(own[...])
    xh = jnp.concatenate([th, oh])
    xl = jnp.concatenate([tl, ol])
    y = dot(l1[0], xh) + dot(l1[0], xl) + dot(l1[1], xh)
    yr, yi = y[:512], y[512:]
    c, s = tw1[0], tw1[1]
    yr, yi = yr * c - yi * s, yr * s + yi * c
    rh, rl = split2(yr)
    ih, il = split2(yi)
    f = dot(jnp.concatenate([rh, ih, rl, il, rh, ih], 1), m2[...])
    fr, fi = f[:, :128], f[:, 128:]
    c, s = tj[0, 0], tj[0, 1]
    gr, gi = fr * c - fi * s, fr * s + fi * c
    for d in range(16):
        out[d, 0:32, :] = gr[32 * d : 32 * d + 32]
        out[d, 32:64, :] = gi[32 * d : 32 * d + 32]
        out[d, 64:80, :] = extra[d]


def fwd_call(me, tail, own, l1, tw1, m2, tj, extra):
    def whole(x):
        return pl.BlockSpec(x.shape, lambda i, m, n=x.ndim: (0,) * n)

    return pl.pallas_call(
        fwd_kernel,
        grid_spec=pltpu.PrefetchScalarGridSpec(
            num_scalar_prefetch=1,
            grid=(1,),
            in_specs=[
                whole(tail),
                whole(own),
                whole(l1),
                whole(tw1),
                whole(m2),
                pl.BlockSpec((1, 2, 512, 128), lambda i, m: (m[0], 0, 0, 0)),
                whole(extra),
            ],
            out_specs=pl.BlockSpec((16, 80, 128), lambda i, m: (0, 0, 0)),
        ),
        out_shape=jax.ShapeDtypeStruct((16, 80, 128), F32),
        compiler_params=pltpu.CompilerParams(vmem_limit_bytes=FWD_VMEM),
    )(me, tail, own, l1, tw1, m2, tj, extra)


def swap_groups(x):
    row = lax.broadcasted_iota(jnp.int32, x.shape, 0)
    lane = lax.broadcasted_iota(jnp.int32, x.shape, 1)
    n = x.shape[0]
    for t in range(3):
        d, w = 1 << t, 1 << SWAP[t]
        rb, lb = (row >> t) & 1, (lane >> SWAP[t]) & 1
        up = pltpu.roll(pltpu.roll(x, d, 0), 128 - w, 1)
        dn = pltpu.roll(pltpu.roll(x, n - d, 0), w, 1)
        x = jnp.where(rb == lb, x, jnp.where(rb == 1, up, dn))
    return x


def swap_low_bits(v):
    lane = lax.broadcasted_iota(jnp.int32, v[0].shape, 1)
    v = list(v)
    for t in range(3):
        w = 1 << t
        clear = (lane >> t) & 1 == 0
        for i in range(8):
            if not i & w:
                p, q = v[i], v[i | w]
                v[i] = jnp.where(clear, p, pltpu.roll(q, w, 1))
                v[i | w] = jnp.where(clear, pltpu.roll(p, 128 - w, 1), q)
    return v


def mix_kernel(p, w_out, sig_out):
    g = []
    for b in range(4):
        rows = [64 + 80 * (i >> 2) + 4 * (i & 3) + b for i in range(8)]
        g.append(swap_low_bits([p[pl.ds(r, 8, stride=160), :] for r in rows]))
    quarters = []
    for n in range(4):
        rows = [80 * (n + 4 * q) for q in range(4)]
        quarters.append(fft4([(p[i + 32 : i + 64, :], p[i : i + 32, :]) for i in rows]))
    for ah in range(6):
        z = [cmul(quarters[n][ah % 4], n * ah, 16) for n in range(4)]
        im, re = add(add(z[0], z[1]), add(z[2], z[3]))
        re, im = swap_groups(re), swap_groups(im)
        for b in range(4):
            at = slice(8 * b, 8 * b + 8)
            w_out[b, 8 * ah : 8 * ah + 8, :] = re[at] * g[b][ah]
            w_out[b, 48 + 8 * ah : 56 + 8 * ah, :] = im[at] * g[b][ah]
    sig = jnp.sum(g[0][6], keepdims=True) * (1.0 / 64.0)
    sig_out[...] = jnp.broadcast_to(lax.rsqrt(sig), (8, 128))


def mix_call(p):
    return pl.pallas_call(
        mix_kernel,
        out_shape=[
            jax.ShapeDtypeStruct((4, 96, 128), F32),
            jax.ShapeDtypeStruct((8, 128), F32),
        ],
        compiler_params=pltpu.CompilerParams(vmem_limit_bytes=16 << 20),
    )(p)


def inv_kernel(me, w, phi, psi, tw, twb, tw3, e1, e2, *rest):
    h_out = rest[-1]
    core = me[0] & 1
    for u in range(8):
        at = (u // 4 ^ core) * 4 + u % 4
        wr, wi = w[0, at, 0:48, :], w[0, at, 48:96, :]
        v = []
        for m in range(2):
            pc, ps = phi[0, u, 2 * m : 2 * m + 1, :], phi[0, u, 2 * m + 1 : 2 * m + 2, :]
            lane = 16 * m + u
            qc, qs = psi[0, :, lane : lane + 1], psi[0, :, lane + 8 : lane + 9]
            c, s = pc * qc - ps * qs, pc * qs + ps * qc
            v.append(jnp.concatenate([wr * c - wi * s, wr * s + wi * c]))
        vh, vl = split2(jnp.concatenate(v, 1))
        g = lax.dot_general(
            jnp.concatenate([vh, vl, vh]),
            e1[...],
            (((0,), (0,)), ((), ())),
            preferred_element_type=F32,
        )
        fc, fs, bc, bs = tw[0], tw[1], twb[u, 0:1, :], twb[u, 1:2, :]
        c, s = fc * bc - fs * bs, fc * bs + fs * bc
        zr, zi = [], []
        for m in range(2):
            gr, gi = g[128 * m : 128 * m + 128, :128], g[128 * m : 128 * m + 128, 128:]
            zr.append(gr * c - gi * s)
            zi.append(gr * s + gi * c)
        z = jnp.concatenate([jnp.concatenate(zr, 1), jnp.concatenate(zi, 1)], 0)
        zh, zl = split2(z)
        h = dot(e2[...], jnp.concatenate([zh, zl, zh], 0))
        c, s = tw3[0, :, u : u + 1], tw3[0, :, u + 8 : u + 9]
        hr, hi = h[:128], h[128:]
        h_out[:, u, 0] = (hr * c - hi * s).reshape(16, 8, 256)
        h_out[:, u, 1] = (hr * s + hi * c).reshape(16, 8, 256)


def inv_call(me, w, chips, ph, t, prev):
    count = len(chips)

    def chip(i, m):
        y, x = m[0] >> 3, (m[0] >> 1) & 3
        dy, dx = chips[0]
        for n in range(1, count):
            dy = jnp.where(i == n, chips[n][0], dy)
            dx = jnp.where(i == n, chips[n][1], dx)
        return ((y + dy) & 1) * 4 + ((x + dx) & 3)

    in_specs = [
        pl.BlockSpec((1, 8, 96, 128), lambda i, m: (i, 0, 0, 0)),
        pl.BlockSpec((1, 8, 4, 128), lambda i, m: (chip(i, m), 0, 0, 0)),
        pl.BlockSpec((1, 48, 128), lambda i, m: (chip(i, m), 0, 0)),
        pl.BlockSpec((2, 128, 128), lambda i, m: (0, 0, 0)),
        pl.BlockSpec((8, 2, 128), lambda i, m: (chip(i, m), 0, 0)),
        pl.BlockSpec((1, 128, 128), lambda i, m: (chip(i, m), 0, 0)),
        pl.BlockSpec((288, 256), lambda i, m: (0, 0)),
        pl.BlockSpec((256, 768), lambda i, m: (0, 0)),
    ]
    args = [me, w, *ph, t["tw"], t["twb"], t["tw3"], t["e1"], t["e2"]]
    alias = {}
    if prev is not None:
        in_specs.append(pl.BlockSpec(memory_space=pl.ANY))
        args.append(prev)
        alias = {9: 0}
    return pl.pallas_call(
        inv_kernel,
        grid_spec=pltpu.PrefetchScalarGridSpec(
            num_scalar_prefetch=1,
            grid=(count,),
            in_specs=in_specs,
            out_specs=pl.BlockSpec(
                (16, 8, 2, 8, 256), lambda i, m: (0, chip(i, m), 0, 0, 0)
            ),
        ),
        out_shape=jax.ShapeDtypeStruct((16, 64, 2, 8, 256), F32),
        input_output_aliases=alias,
        compiler_params=pltpu.CompilerParams(vmem_limit_bytes=INV_VMEM),
        cost_estimate=pl.CostEstimate(
            flops=count * 1_500_000_000, bytes_accessed=count * 3_000_000, transcendentals=0
        ),
    )(*args)


def cmul(x, num, den):
    num %= den
    re, im = x
    if num == 0:
        return re, im
    if 4 * num == den:
        return -im, re
    if 2 * num == den:
        return -re, -im
    if 4 * num == 3 * den:
        return im, -re
    c = float(math.cos(2 * math.pi * num / den))
    s = float(math.sin(2 * math.pi * num / den))
    if (8 * num) % den == 0:
        r = math.sqrt(0.5)
        a = r if c > 0 else -r
        b = r if s > 0 else -r
        if a == b:
            return a * (re - im), a * (re + im)
        return a * (re + im), a * (im - re)
    return re * c - im * s, re * s + im * c


def add(x, y):
    return x[0] + y[0], x[1] + y[1]


def sub(x, y):
    return x[0] - y[0], x[1] - y[1]


def fft4(x):
    p, q = add(x[0], x[2]), sub(x[0], x[2])
    r, s = add(x[1], x[3]), sub(x[1], x[3])
    s = (-s[1], s[0])
    return [add(p, r), add(q, s), sub(p, r), sub(q, s)]


def out_kernel(h, sig, out, mid):
    scale = sig[...]
    for m in range(2):
        at = slice(128 * m, 128 * m + 128)
        for lo in range(8):
            x = [(h[0, 8 * hi + lo, 0, :, at], h[0, 8 * hi + lo, 1, :, at]) for hi in range(8)]
            ev, od = fft4(x[0::2]), fft4(x[1::2])
            for f in range(4):
                o = cmul(od[f], f, 8)
                for f2, v in ((f, add(ev[f], o)), (f + 4, sub(ev[f], o))):
                    v = cmul(v, lo * f2, 64)
                    mid[f2, lo, 0] = v[0]
                    mid[f2, lo, 1] = v[1]
        for f2 in range(8):
            x = [(mid[f2, lo, 0], mid[f2, lo, 1]) for lo in range(8)]
            ev, od = fft4(x[0::2]), fft4(x[1::2])
            for f in range(4):
                v = sub(ev[f], cmul(od[f], f, 8))
                power = v[0] * v[0] + v[1] * v[1]
                mag = power * lax.rsqrt(jnp.maximum(power, 1e-37)) * scale
                out[f2 + 8 * f, pl.ds(m, 8, stride=2), :] = mag


def out_call(h, sig):
    return pl.pallas_call(
        out_kernel,
        grid=(16,),
        in_specs=[
            pl.BlockSpec((1, 64, 2, 8, 256), lambda i: (i, 0, 0, 0, 0)),
            pl.BlockSpec((8, 128), lambda i: (0, 0)),
        ],
        out_specs=pl.BlockSpec((32, 16, 128), lambda i: (0, i, 0)),
        out_shape=jax.ShapeDtypeStruct((32, 256, 128), F32),
        scratch_shapes=[pltpu.VMEM((8, 8, 2, 8, 128), F32)],
        compiler_params=pltpu.CompilerParams(vmem_limit_bytes=OUT_VMEM),
    )(h, sig)


def place(y, x, c):
    return (y % 2 * 4 + x % 4) * 2 + c


def sent(v, dy, dx, dc):
    route = [
        (place(y, x, c), place(y + dy, x + dx, (c + dc) % 2))
        for y in range(2)
        for x in range(4)
        for c in range(2)
    ]
    return lax.ppermute(v, "tmpl", route)


def phases(chirp_slope, chirp_curve):
    row = jnp.arange(4, dtype=jnp.int32)[None, :, None]
    s = jnp.where(row < 2, chirp_slope[0], chirp_slope[1])
    c = jnp.where(row < 2, chirp_curve[0], chirp_curve[1])
    b = 64 * B1[None, None, :] + np.arange(64)[:, None, None]
    square = jnp.asarray(b * b % N, jnp.int32)
    p = (s * jnp.asarray(b, jnp.int32) + c * square - (N // 4) * (row % 2)) % N
    phi = jnp.cos(p.astype(F32) * (2 * math.pi / N))
    lane = jnp.arange(128, dtype=jnp.int32)[None, None, :]
    s = jnp.where(lane < 16, chirp_slope[0], chirp_slope[1])
    c = jnp.where(lane < 16, chirp_curve[0], chirp_curve[1])
    b0 = 8 * jnp.arange(8, dtype=jnp.int32)[:, None, None] + lane % 8
    a = jnp.arange(48, dtype=jnp.int32)[None, :, None]
    p = (a * ((s + 2 * c * b0) % 128) - 32 * (lane // 8 % 2)) % 128
    psi = jnp.cos(p.astype(F32) * (2 * math.pi / 128))
    return phi.reshape(8, 8, 4, 128), psi


def local(strain, psd_bins, psd_values, chirp_slope, chirp_curve):
    t = {k: jnp.asarray(v) for k, v in tables().items()}
    member = lax.axis_index("tmpl")
    me = member.astype(jnp.int32).reshape(1)
    own = strain.reshape(256, 128)
    count = lax.axis_size("tm")
    tail = lax.ppermute(own, "tm", [(i, i + 1) for i in range(count - 1)])

    extra = psd_call(me, psd_bins, psd_values.reshape(64, 128))
    sent_out = fwd_call(me, tail, own, t["l1"], t["tw1"], t["m2"], t["tj"], extra)
    sent_out, chirp_slope, chirp_curve = lax.optimization_barrier(
        (sent_out, chirp_slope, chirp_curve)
    )
    parts = lax.all_to_all(sent_out, "tmpl", split_axis=0, concat_axis=0, tiled=True)
    ph = phases(chirp_slope, chirp_curve)
    parts, *ph = lax.optimization_barrier((parts, *ph))
    w, scale = mix_call(parts.reshape(1280, 128))

    def work(blocks, chips, prev):
        mine = jnp.stack(blocks)
        both = jnp.concatenate([mine, sent(mine, 0, 0, 1)], 1)
        return inv_call(me, both, chips, ph, t, prev)

    up = sent(w, 1, 0, 0)
    right = sent(w, 0, 1, 0)
    left = sent(w, 0, -1, 0)
    h = work([w], [(0, 0)], None)
    up, right, left, h = lax.optimization_barrier((up, right, left, h))
    right2 = sent(jnp.concatenate([up, right[:2]]), 0, 1, 0)
    left2 = sent(jnp.concatenate([up, left[2:]]), 0, -1, 0)
    h = work([up, right, left], [(1, 0), (0, -1), (0, 1)], h)
    right2, left2, h = lax.optimization_barrier((right2, left2, h))
    right3 = sent(right2[:2], 0, 1, 0)
    left3 = sent(left2[2:4], 0, -1, 0)
    far = jnp.concatenate([right2[4:], left2[4:]])
    h = work([right2[:4], left2[:4]], [(1, -1), (1, 1)], h)
    right3, left3, h = lax.optimization_barrier((right3, left3, h))
    h = work([far], [(0, 2)], h)
    h = work([jnp.concatenate([right3, left3])], [(1, 2)], h)
    out = out_call(h, scale)
    return out.reshape(4096, 2, 128).transpose(1, 0, 2).reshape(2, 4096 * 128)


def solution(mesh):
    placed = (P("tmpl", "tm"), P(None, "tmpl"), P("tm", None), P("tmpl"), P("tmpl"))
    return jax.shard_map(
        local, mesh=mesh, in_specs=placed, out_specs=P("tmpl", "tm"), check_vma=False
    )
```

```python
import functools
import math

import jax
import jax.numpy as jnp
import ml_dtypes
import numpy as np
from jax import lax
from jax.experimental import pallas as pl
from jax.experimental.pallas import tpu as pltpu
from jax.sharding import PartitionSpec as P

N = 1 << 20
K_LOW = N // 200
BF = jnp.bfloat16
F32 = jnp.float32
INV_VMEM = 24 << 20
FWD_VMEM = 58 << 20
OUT_VMEM = 24 << 20


def halves(x):
    x = np.asarray(x, np.float32)
    hi = x.astype(ml_dtypes.bfloat16)
    lo = (x - hi.astype(np.float32)).astype(ml_dtypes.bfloat16)
    return hi, lo


def unit(num, den, sign):
    ang = (num % den) * (sign * 2.0 * math.pi / den)
    return np.cos(ang), np.sin(ang)


LANE = np.arange(128)


def bits(x, *order):
    out = 0 * x
    for b in order:
        out = 2 * out + (x >> b & 1)
    return out


B1 = bits(LANE, 2, 1, 6, 5, 4, 3, 0)
SWAP = (0, 3, 4)


@functools.lru_cache(None)
def tables():
    t = {}
    rows = np.arange(512)
    low = rows // 8 + 64 * (rows % 8)
    c, s = unit(low[:, None] * np.arange(512)[None, :], 512, -1)
    hi, lo = halves(np.concatenate([c, s]))
    t["l1"] = np.stack([hi, lo])
    c, s = unit(low[:, None] * LANE[None, :], 65536, -1)
    t["tw1"] = np.stack([c, s]).astype(np.float32)
    top = 16 * bits(LANE, 4, 3, 0) + (B1 >> 3)
    c, s = unit(LANE[:, None] * top[None, :], 128, -1)
    hi, lo = halves(np.block([[c, s], [-s, c]]))
    t["m2"] = np.concatenate([hi, hi, lo])
    q = low[:, None] + 512 * top[None, :]
    c, s = unit(np.arange(16)[:, None, None] * q[None], N, -1)
    t["tj"] = np.stack([c, s], 1).astype(np.float32)
    a = np.arange(48)
    c, s = unit(a[:, None] * LANE[None, :], 128, 1)
    hi, lo = halves(np.block([[c, s], [-s, c]]))
    t["e1"] = np.concatenate([hi, hi, lo])
    c, s = unit(LANE[:, None] * B1[None, :], 128, 1)
    hi, lo = halves(np.block([[c, -s], [s, c]]))
    t["e2"] = np.concatenate([hi, hi, lo], 1)
    c, s = unit(64 * B1[:, None] * LANE[None, :], N, 1)
    t["tw"] = np.stack([c, s]).astype(np.float32)
    c, s = unit(np.arange(64)[:, None] * LANE[None, :], N, 1)
    t["twb"] = np.stack([c, s], 1).astype(np.float32)
    c, s = unit(np.arange(64)[:, None] * LANE[None, :], 8192, 1)
    t3 = np.zeros((8, 128, 128), np.float32)
    t3[:, :, 0:8] = c.reshape(8, 8, 128).transpose(0, 2, 1)
    t3[:, :, 8:16] = s.reshape(8, 8, 128).transpose(0, 2, 1)
    t["tw3"] = t3
    return t


def split2(x):
    hi = x.astype(BF)
    lo = (x - hi.astype(F32)).astype(BF)
    return hi, lo


def dot(a, b):
    return jnp.dot(a, b, preferred_element_type=F32)


def psd_kernel(me, bins_hbm, vals_hbm, out, g, tr, bins, vals, sems):
    fetch = [
        pltpu.make_async_copy(bins_hbm, bins, sems.at[0]),
        pltpu.make_async_copy(vals_hbm, vals, sems.at[1]),
    ]
    for copy in fetch:
        copy.start()
    row = lax.broadcasted_iota(jnp.int32, (256, 128), 0)
    lane = lax.broadcasted_iota(jnp.int32, (256, 128), 1)
    k = (row & 7) * 65536 + me[0] * 4096 + (row >> 3) * 128 + lane
    ratio = jnp.maximum(k.astype(F32) / K_LOW, 1.0)
    amp = jnp.where(k >= K_LOW, jnp.exp(jnp.log(ratio) * (-7.0 / 6.0)), 0.0)
    for copy in fetch:
        copy.wait()
    v0 = vals[...]
    p0 = v0.astype(BF)
    v1 = v0 - p0.astype(F32)
    p1 = v1.astype(BF)
    p2 = (v1 - p1.astype(F32)).astype(BF)
    parts = jnp.concatenate([p0, p1, p2])
    width = 512
    low = lax.broadcasted_iota(jnp.int32, (128, width), 0)
    high = lax.broadcasted_iota(jnp.int32, (64, width), 0)
    g[...] = jnp.ones((256, 128), F32)

    def chunk(i, carry):
        at = pl.multiple_of(i * width, width)
        idx = bins[:, pl.ds(at, width)]
        for ah in range(6):
            one = idx[ah : ah + 1]
            hot = jnp.where((one & 127) == low, 1.0, 0.0).astype(BF)
            got = dot(parts, hot)
            got = got[:64] + got[64:128] + got[128:]
            got = jnp.sum(jnp.where((one >> 7) == high, got, 0.0), axis=0, keepdims=True)
            for q in range(width // 128):
                g[pl.ds(i * (width // 16) + 8 * q + ah, 1), :] = got[:, 128 * q : 128 * q + 128]
        return carry

    lax.fori_loop(0, 4096 // width, chunk, 0)
    f = amp / g[...]
    rows = (row & 7) < 6
    share = jnp.sum(jnp.where(rows, f * amp, 0.0), keepdims=True)
    full = jnp.where(rows, f * (1.0 / 1024.0), jnp.broadcast_to(share, (256, 128)))
    for half in range(2):
        tr[...] = full[128 * half : 128 * half + 128].T
        for low_bit in range(2):
            for d in range(16):
                at = 8 * half + 4 * low_bit
                src = 64 * low_bit + 4 * d
                out[d, at : at + 4, :] = tr[src : src + 4, :]


def psd_call(me, bins, vals):
    return pl.pallas_call(
        psd_kernel,
        grid_spec=pltpu.PrefetchScalarGridSpec(
            num_scalar_prefetch=1,
            grid=(1,),
            in_specs=[pl.BlockSpec(memory_space=pl.ANY)] * 2,
            out_specs=pl.BlockSpec((16, 16, 128), lambda i, m: (0, 0, 0)),
            scratch_shapes=[
                pltpu.VMEM((256, 128), F32),
                pltpu.VMEM((128, 128), F32),
                pltpu.VMEM((8, 4096), jnp.int32),
                pltpu.VMEM((64, 128), F32),
                pltpu.SemaphoreType.DMA((2,)),
            ],
        ),
        out_shape=jax.ShapeDtypeStruct((16, 16, 128), F32),
        compiler_params=pltpu.CompilerParams(vmem_limit_bytes=60 << 20),
    )(me, bins, vals)


def fwd_kernel(me, tail, own, l1, tw1, m2, tj, extra, out):
    th, tl = split2(tail[...])
    oh, ol = split2(own[...])
    xh = jnp.concatenate([th, oh])
    xl = jnp.concatenate([tl, ol])
    y = dot(l1[0], xh) + dot(l1[0], xl) + dot(l1[1], xh)
    yr, yi = y[:512], y[512:]
    c, s = tw1[0], tw1[1]
    yr, yi = yr * c - yi * s, yr * s + yi * c
    rh, rl = split2(yr)
    ih, il = split2(yi)
    f = dot(jnp.concatenate([rh, ih, rl, il, rh, ih], 1), m2[...])
    fr, fi = f[:, :128], f[:, 128:]
    c, s = tj[0, 0], tj[0, 1]
    gr, gi = fr * c - fi * s, fr * s + fi * c
    for d in range(16):
        out[d, 0:32, :] = gr[32 * d : 32 * d + 32]
        out[d, 32:64, :] = gi[32 * d : 32 * d + 32]
        out[d, 64:80, :] = extra[d]


def fwd_call(me, tail, own, l1, tw1, m2, tj, extra):
    def whole(x):
        return pl.BlockSpec(x.shape, lambda i, m, n=x.ndim: (0,) * n)

    return pl.pallas_call(
        fwd_kernel,
        grid_spec=pltpu.PrefetchScalarGridSpec(
            num_scalar_prefetch=1,
            grid=(1,),
            in_specs=[
                whole(tail),
                whole(own),
                whole(l1),
                whole(tw1),
                whole(m2),
                pl.BlockSpec((1, 2, 512, 128), lambda i, m: (m[0], 0, 0, 0)),
                whole(extra),
            ],
            out_specs=pl.BlockSpec((16, 80, 128), lambda i, m: (0, 0, 0)),
        ),
        out_shape=jax.ShapeDtypeStruct((16, 80, 128), F32),
        compiler_params=pltpu.CompilerParams(vmem_limit_bytes=FWD_VMEM),
    )(me, tail, own, l1, tw1, m2, tj, extra)


def swap_groups(x):
    row = lax.broadcasted_iota(jnp.int32, x.shape, 0)
    lane = lax.broadcasted_iota(jnp.int32, x.shape, 1)
    n = x.shape[0]
    for t in range(3):
        d, w = 1 << t, 1 << SWAP[t]
        rb, lb = (row >> t) & 1, (lane >> SWAP[t]) & 1
        up = pltpu.roll(pltpu.roll(x, d, 0), 128 - w, 1)
        dn = pltpu.roll(pltpu.roll(x, n - d, 0), w, 1)
        x = jnp.where(rb == lb, x, jnp.where(rb == 1, up, dn))
    return x


def swap_low_bits(v):
    lane = lax.broadcasted_iota(jnp.int32, v[0].shape, 1)
    v = list(v)
    for t in range(3):
        w = 1 << t
        clear = (lane >> t) & 1 == 0
        for i in range(8):
            if not i & w:
                p, q = v[i], v[i | w]
                v[i] = jnp.where(clear, p, pltpu.roll(q, w, 1))
                v[i | w] = jnp.where(clear, pltpu.roll(p, 128 - w, 1), q)
    return v


def mix_kernel(p, w_out, sig_out):
    g = []
    for b in range(4):
        rows = [64 + 80 * (i >> 2) + 4 * (i & 3) + b for i in range(8)]
        g.append(swap_low_bits([p[pl.ds(r, 8, stride=160), :] for r in rows]))
    quarters = []
    for n in range(4):
        rows = [80 * (n + 4 * q) for q in range(4)]
        quarters.append(fft4([(p[i + 32 : i + 64, :], p[i : i + 32, :]) for i in rows]))
    for ah in range(6):
        z = [cmul(quarters[n][ah % 4], n * ah, 16) for n in range(4)]
        im, re = add(add(z[0], z[1]), add(z[2], z[3]))
        re, im = swap_groups(re), swap_groups(im)
        for b in range(4):
            at = slice(8 * b, 8 * b + 8)
            w_out[b, 8 * ah : 8 * ah + 8, :] = re[at] * g[b][ah]
            w_out[b, 48 + 8 * ah : 56 + 8 * ah, :] = im[at] * g[b][ah]
    sig = jnp.sum(g[0][6], keepdims=True) * (1.0 / 64.0)
    sig_out[...] = jnp.broadcast_to(lax.rsqrt(sig), (8, 128))


def mix_call(p):
    return pl.pallas_call(
        mix_kernel,
        out_shape=[
            jax.ShapeDtypeStruct((4, 96, 128), F32),
            jax.ShapeDtypeStruct((8, 128), F32),
        ],
        compiler_params=pltpu.CompilerParams(vmem_limit_bytes=16 << 20),
    )(p)


def inv_kernel(me, w, phi, psi, tw, twb, tw3, e1, e2, *rest):
    h_out = rest[-1]
    core = me[0] & 1
    for u in range(8):
        at = (u // 4 ^ core) * 4 + u % 4
        wr, wi = w[0, at, 0:48, :], w[0, at, 48:96, :]
        v = []
        for m in range(2):
            pc, ps = phi[0, u, 2 * m : 2 * m + 1, :], phi[0, u, 2 * m + 1 : 2 * m + 2, :]
            lane = 16 * m + u
            qc, qs = psi[0, :, lane : lane + 1], psi[0, :, lane + 8 : lane + 9]
            c, s = pc * qc - ps * qs, pc * qs + ps * qc
            v.append(jnp.concatenate([wr * c - wi * s, wr * s + wi * c]))
        vh, vl = split2(jnp.concatenate(v, 1))
        g = lax.dot_general(
            jnp.concatenate([vh, vl, vh]),
            e1[...],
            (((0,), (0,)), ((), ())),
            preferred_element_type=F32,
        )
        fc, fs, bc, bs = tw[0], tw[1], twb[u, 0:1, :], twb[u, 1:2, :]
        c, s = fc * bc - fs * bs, fc * bs + fs * bc
        zr, zi = [], []
        for m in range(2):
            gr, gi = g[128 * m : 128 * m + 128, :128], g[128 * m : 128 * m + 128, 128:]
            zr.append(gr * c - gi * s)
            zi.append(gr * s + gi * c)
        z = jnp.concatenate([jnp.concatenate(zr, 1), jnp.concatenate(zi, 1)], 0)
        zh, zl = split2(z)
        h = dot(e2[...], jnp.concatenate([zh, zl, zh], 0))
        c, s = tw3[0, :, u : u + 1], tw3[0, :, u + 8 : u + 9]
        hr, hi = h[:128], h[128:]
        h_out[:, u, 0] = (hr * c - hi * s).reshape(16, 8, 256)
        h_out[:, u, 1] = (hr * s + hi * c).reshape(16, 8, 256)


def inv_call(me, w, chips, ph, t, prev):
    count = len(chips)

    def chip(i, m):
        y, x = m[0] >> 3, (m[0] >> 1) & 3
        dy, dx = chips[0]
        for n in range(1, count):
            dy = jnp.where(i == n, chips[n][0], dy)
            dx = jnp.where(i == n, chips[n][1], dx)
        return ((y + dy) & 1) * 4 + ((x + dx) & 3)

    in_specs = [
        pl.BlockSpec((1, 8, 96, 128), lambda i, m: (i, 0, 0, 0)),
        pl.BlockSpec((1, 8, 4, 128), lambda i, m: (chip(i, m), 0, 0, 0)),
        pl.BlockSpec((1, 48, 128), lambda i, m: (chip(i, m), 0, 0)),
        pl.BlockSpec((2, 128, 128), lambda i, m: (0, 0, 0)),
        pl.BlockSpec((8, 2, 128), lambda i, m: (chip(i, m), 0, 0)),
        pl.BlockSpec((1, 128, 128), lambda i, m: (chip(i, m), 0, 0)),
        pl.BlockSpec((288, 256), lambda i, m: (0, 0)),
        pl.BlockSpec((256, 768), lambda i, m: (0, 0)),
    ]
    args = [me, w, *ph, t["tw"], t["twb"], t["tw3"], t["e1"], t["e2"]]
    alias = {}
    if prev is not None:
        in_specs.append(pl.BlockSpec(memory_space=pl.ANY))
        args.append(prev)
        alias = {9: 0}
    return pl.pallas_call(
        inv_kernel,
        grid_spec=pltpu.PrefetchScalarGridSpec(
            num_scalar_prefetch=1,
            grid=(count,),
            in_specs=in_specs,
            out_specs=pl.BlockSpec(
                (16, 8, 2, 8, 256), lambda i, m: (0, chip(i, m), 0, 0, 0)
            ),
        ),
        out_shape=jax.ShapeDtypeStruct((16, 64, 2, 8, 256), F32),
        input_output_aliases=alias,
        compiler_params=pltpu.CompilerParams(vmem_limit_bytes=INV_VMEM),
        cost_estimate=pl.CostEstimate(
            flops=count * 1_500_000_000, bytes_accessed=count * 3_000_000, transcendentals=0
        ),
    )(*args)


def cmul(x, num, den):
    num %= den
    re, im = x
    if num == 0:
        return re, im
    if 4 * num == den:
        return -im, re
    if 2 * num == den:
        return -re, -im
    if 4 * num == 3 * den:
        return im, -re
    c = float(math.cos(2 * math.pi * num / den))
    s = float(math.sin(2 * math.pi * num / den))
    if (8 * num) % den == 0:
        r = math.sqrt(0.5)
        a = r if c > 0 else -r
        b = r if s > 0 else -r
        if a == b:
            return a * (re - im), a * (re + im)
        return a * (re + im), a * (im - re)
    return re * c - im * s, re * s + im * c


def add(x, y):
    return x[0] + y[0], x[1] + y[1]


def sub(x, y):
    return x[0] - y[0], x[1] - y[1]


def fft4(x):
    p, q = add(x[0], x[2]), sub(x[0], x[2])
    r, s = add(x[1], x[3]), sub(x[1], x[3])
    s = (-s[1], s[0])
    return [add(p, r), add(q, s), sub(p, r), sub(q, s)]


def out_kernel(h, sig, out, mid):
    scale = sig[...]
    for m in range(2):
        at = slice(128 * m, 128 * m + 128)
        for lo in range(8):
            x = [(h[0, 8 * hi + lo, 0, :, at], h[0, 8 * hi + lo, 1, :, at]) for hi in range(8)]
            ev, od = fft4(x[0::2]), fft4(x[1::2])
            for f in range(4):
                o = cmul(od[f], f, 8)
                for f2, v in ((f, add(ev[f], o)), (f + 4, sub(ev[f], o))):
                    v = cmul(v, lo * f2, 64)
                    mid[f2, lo, 0] = v[0]
                    mid[f2, lo, 1] = v[1]
        for f2 in range(8):
            x = [(mid[f2, lo, 0], mid[f2, lo, 1]) for lo in range(8)]
            ev, od = fft4(x[0::2]), fft4(x[1::2])
            for f in range(4):
                v = sub(ev[f], cmul(od[f], f, 8))
                power = v[0] * v[0] + v[1] * v[1]
                mag = power * lax.rsqrt(jnp.maximum(power, 1e-37)) * scale
                out[f2 + 8 * f, pl.ds(m, 8, stride=2), :] = mag


def out_call(h, sig):
    return pl.pallas_call(
        out_kernel,
        grid=(16,),
        in_specs=[
            pl.BlockSpec((1, 64, 2, 8, 256), lambda i: (i, 0, 0, 0, 0)),
            pl.BlockSpec((8, 128), lambda i: (0, 0)),
        ],
        out_specs=pl.BlockSpec((32, 16, 128), lambda i: (0, i, 0)),
        out_shape=jax.ShapeDtypeStruct((32, 256, 128), F32),
        scratch_shapes=[pltpu.VMEM((8, 8, 2, 8, 128), F32)],
        compiler_params=pltpu.CompilerParams(vmem_limit_bytes=OUT_VMEM),
    )(h, sig)


def place(y, x, c):
    return (y % 2 * 4 + x % 4) * 2 + c


def sent(v, dy, dx, dc):
    route = [
        (place(y, x, c), place(y + dy, x + dx, (c + dc) % 2))
        for y in range(2)
        for x in range(4)
        for c in range(2)
    ]
    return lax.ppermute(v, "tmpl", route)


def phases(chirp_slope, chirp_curve):
    row = jnp.arange(4, dtype=jnp.int32)[None, :, None]
    s = jnp.where(row < 2, chirp_slope[0], chirp_slope[1])
    c = jnp.where(row < 2, chirp_curve[0], chirp_curve[1])
    b = 64 * B1[None, None, :] + np.arange(64)[:, None, None]
    square = jnp.asarray(b * b % N, jnp.int32)
    p = (s * jnp.asarray(b, jnp.int32) + c * square - (N // 4) * (row % 2)) % N
    phi = jnp.cos(p.astype(F32) * (2 * math.pi / N))
    lane = jnp.arange(128, dtype=jnp.int32)[None, None, :]
    s = jnp.where(lane < 16, chirp_slope[0], chirp_slope[1])
    c = jnp.where(lane < 16, chirp_curve[0], chirp_curve[1])
    b0 = 8 * jnp.arange(8, dtype=jnp.int32)[:, None, None] + lane % 8
    a = jnp.arange(48, dtype=jnp.int32)[None, :, None]
    p = (a * ((s + 2 * c * b0) % 128) - 32 * (lane // 8 % 2)) % 128
    psi = jnp.cos(p.astype(F32) * (2 * math.pi / 128))
    return phi.reshape(8, 8, 4, 128), psi


def local(strain, psd_bins, psd_values, chirp_slope, chirp_curve):
    t = {k: jnp.asarray(v) for k, v in tables().items()}
    member = lax.axis_index("tmpl")
    me = member.astype(jnp.int32).reshape(1)
    own = strain.reshape(256, 128)
    count = lax.axis_size("tm")
    tail = lax.ppermute(own, "tm", [(i, i + 1) for i in range(count - 1)])

    extra = psd_call(me, psd_bins, psd_values.reshape(64, 128))
    sent_out = fwd_call(me, tail, own, t["l1"], t["tw1"], t["m2"], t["tj"], extra)
    sent_out, chirp_slope, chirp_curve = lax.optimization_barrier(
        (sent_out, chirp_slope, chirp_curve)
    )
    parts = lax.all_to_all(sent_out, "tmpl", split_axis=0, concat_axis=0, tiled=True)
    ph = phases(chirp_slope, chirp_curve)
    parts, *ph = lax.optimization_barrier((parts, *ph))
    w, scale = mix_call(parts.reshape(1280, 128))

    def work(blocks, chips, prev):
        mine = jnp.stack(blocks)
        both = jnp.concatenate([mine, sent(mine, 0, 0, 1)], 1)
        return inv_call(me, both, chips, ph, t, prev)

    up = sent(w, 1, 0, 0)
    right = sent(w, 0, 1, 0)
    left = sent(w, 0, -1, 0)
    h = work([w], [(0, 0)], None)
    up, right, left, h = lax.optimization_barrier((up, right, left, h))
    right2 = sent(jnp.concatenate([up, right[:2]]), 0, 1, 0)
    left2 = sent(jnp.concatenate([up, left[2:]]), 0, -1, 0)
    h = work([up, right, left], [(1, 0), (0, -1), (0, 1)], h)
    right2, left2, h = lax.optimization_barrier((right2, left2, h))
    right3 = sent(right2[:2], 0, 1, 0)
    left3 = sent(left2[2:4], 0, -1, 0)
    far = jnp.concatenate([right2[4:], left2[4:]])
    h = work([right2[:4], left2[:4]], [(1, -1), (1, 1)], h)
    right3, left3, h = lax.optimization_barrier((right3, left3, h))
    h = work([far], [(0, 2)], h)
    h = work([jnp.concatenate([right3, left3])], [(1, 2)], h)
    out = out_call(h, scale)
    return out.reshape(4096, 2, 128).transpose(1, 0, 2).reshape(2, 4096 * 128)


def solution(mesh):
    placed = (P("tmpl", "tm"), P(None, "tmpl"), P("tm", None), P("tmpl"), P("tmpl"))
    return jax.shard_map(
        local, mesh=mesh, in_specs=placed, out_specs=P("tmpl", "tm"), check_vma=False
    )
```

```python
import functools
import math

import jax
import jax.numpy as jnp
import ml_dtypes
import numpy as np
from jax import lax
from jax.experimental import pallas as pl
from jax.experimental.pallas import tpu as pltpu
from jax.sharding import PartitionSpec as P

N = 1 << 20
K_LOW = N // 200
BF = jnp.bfloat16
F32 = jnp.float32
INV_VMEM = 24 << 20
FWD_VMEM = 58 << 20
OUT_VMEM = 24 << 20


def halves(x):
    x = np.asarray(x, np.float32)
    hi = x.astype(ml_dtypes.bfloat16)
    lo = (x - hi.astype(np.float32)).astype(ml_dtypes.bfloat16)
    return hi, lo


def unit(num, den, sign):
    ang = (num % den) * (sign * 2.0 * math.pi / den)
    return np.cos(ang), np.sin(ang)


LANE = np.arange(128)


def bits(x, *order):
    out = 0 * x
    for b in order:
        out = 2 * out + (x >> b & 1)
    return out


B1 = bits(LANE, 2, 1, 6, 5, 4, 3, 0)
SWAP = (0, 3, 4)


@functools.lru_cache(None)
def tables():
    t = {}
    rows = np.arange(512)
    low = rows // 8 + 64 * (rows % 8)
    c, s = unit(low[:, None] * np.arange(512)[None, :], 512, -1)
    hi, lo = halves(np.concatenate([c, s]))
    t["l1"] = np.stack([hi, lo])
    c, s = unit(low[:, None] * LANE[None, :], 65536, -1)
    t["tw1"] = np.stack([c, s]).astype(np.float32)
    top = 16 * bits(LANE, 4, 3, 0) + (B1 >> 3)
    c, s = unit(LANE[:, None] * top[None, :], 128, -1)
    hi, lo = halves(np.block([[c, s], [-s, c]]))
    t["m2"] = np.concatenate([hi, hi, lo])
    q = low[:, None] + 512 * top[None, :]
    c, s = unit(np.arange(16)[:, None, None] * q[None], N, -1)
    t["tj"] = np.stack([c, s], 1).astype(np.float32)
    a = np.arange(48)
    c, s = unit(a[:, None] * LANE[None, :], 128, 1)
    hi, lo = halves(np.block([[c, s], [-s, c]]))
    t["e1"] = np.concatenate([hi, hi, lo])
    c, s = unit(LANE[:, None] * B1[None, :], 128, 1)
    hi, lo = halves(np.block([[c, -s], [s, c]]))
    t["e2"] = np.concatenate([hi, hi, lo], 1)
    c, s = unit(64 * B1[:, None] * LANE[None, :], N, 1)
    t["tw"] = np.stack([c, s]).astype(np.float32)
    c, s = unit(np.arange(64)[:, None] * LANE[None, :], N, 1)
    t["twb"] = np.stack([c, s], 1).astype(np.float32)
    c, s = unit(np.arange(64)[:, None] * LANE[None, :], 8192, 1)
    t3 = np.zeros((8, 128, 128), np.float32)
    t3[:, :, 0:8] = c.reshape(8, 8, 128).transpose(0, 2, 1)
    t3[:, :, 8:16] = s.reshape(8, 8, 128).transpose(0, 2, 1)
    t["tw3"] = t3
    return t


def split2(x):
    hi = x.astype(BF)
    lo = (x - hi.astype(F32)).astype(BF)
    return hi, lo


def dot(a, b):
    return jnp.dot(a, b, preferred_element_type=F32)


def psd_kernel(me, bins_hbm, vals_hbm, out, g, tr, bins, vals, sems):
    fetch = [
        pltpu.make_async_copy(bins_hbm, bins, sems.at[0]),
        pltpu.make_async_copy(vals_hbm, vals, sems.at[1]),
    ]
    for copy in fetch:
        copy.start()
    row = lax.broadcasted_iota(jnp.int32, (256, 128), 0)
    lane = lax.broadcasted_iota(jnp.int32, (256, 128), 1)
    k = (row & 7) * 65536 + me[0] * 4096 + (row >> 3) * 128 + lane
    ratio = jnp.maximum(k.astype(F32) / K_LOW, 1.0)
    amp = jnp.where(k >= K_LOW, jnp.exp(jnp.log(ratio) * (-7.0 / 6.0)), 0.0)
    for copy in fetch:
        copy.wait()
    v0 = vals[...]
    p0 = v0.astype(BF)
    v1 = v0 - p0.astype(F32)
    p1 = v1.astype(BF)
    p2 = (v1 - p1.astype(F32)).astype(BF)
    parts = jnp.concatenate([p0, p1, p2])
    width = 512
    low = lax.broadcasted_iota(jnp.int32, (128, width), 0)
    high = lax.broadcasted_iota(jnp.int32, (64, width), 0)
    g[...] = jnp.ones((256, 128), F32)

    def chunk(i, carry):
        at = pl.multiple_of(i * width, width)
        idx = bins[:, pl.ds(at, width)]
        for ah in range(6):
            one = idx[ah : ah + 1]
            hot = jnp.where((one & 127) == low, 1.0, 0.0).astype(BF)
            got = dot(parts, hot)
            got = got[:64] + got[64:128] + got[128:]
            got = jnp.sum(jnp.where((one >> 7) == high, got, 0.0), axis=0, keepdims=True)
            for q in range(width // 128):
                g[pl.ds(i * (width // 16) + 8 * q + ah, 1), :] = got[:, 128 * q : 128 * q + 128]
        return carry

    lax.fori_loop(0, 4096 // width, chunk, 0)
    f = amp / g[...]
    rows = (row & 7) < 6
    share = jnp.sum(jnp.where(rows, f * amp, 0.0), keepdims=True)
    full = jnp.where(rows, f * (1.0 / 1024.0), jnp.broadcast_to(share, (256, 128)))
    for half in range(2):
        tr[...] = full[128 * half : 128 * half + 128].T
        for low_bit in range(2):
            for d in range(16):
                at = 8 * half + 4 * low_bit
                src = 64 * low_bit + 4 * d
                out[d, at : at + 4, :] = tr[src : src + 4, :]


def psd_call(me, bins, vals):
    return pl.pallas_call(
        psd_kernel,
        grid_spec=pltpu.PrefetchScalarGridSpec(
            num_scalar_prefetch=1,
            grid=(1,),
            in_specs=[pl.BlockSpec(memory_space=pl.ANY)] * 2,
            out_specs=pl.BlockSpec((16, 16, 128), lambda i, m: (0, 0, 0)),
            scratch_shapes=[
                pltpu.VMEM((256, 128), F32),
                pltpu.VMEM((128, 128), F32),
                pltpu.VMEM((8, 4096), jnp.int32),
                pltpu.VMEM((64, 128), F32),
                pltpu.SemaphoreType.DMA((2,)),
            ],
        ),
        out_shape=jax.ShapeDtypeStruct((16, 16, 128), F32),
        compiler_params=pltpu.CompilerParams(vmem_limit_bytes=60 << 20),
    )(me, bins, vals)


def fwd_kernel(me, tail, own, l1, tw1, m2, tj, extra, out):
    th, tl = split2(tail[...])
    oh, ol = split2(own[...])
    xh = jnp.concatenate([th, oh])
    xl = jnp.concatenate([tl, ol])
    y = dot(l1[0], xh) + dot(l1[0], xl) + dot(l1[1], xh)
    yr, yi = y[:512], y[512:]
    c, s = tw1[0], tw1[1]
    yr, yi = yr * c - yi * s, yr * s + yi * c
    rh, rl = split2(yr)
    ih, il = split2(yi)
    f = dot(jnp.concatenate([rh, ih, rl, il, rh, ih], 1), m2[...])
    fr, fi = f[:, :128], f[:, 128:]
    c, s = tj[0, 0], tj[0, 1]
    gr, gi = fr * c - fi * s, fr * s + fi * c
    for d in range(16):
        out[d, 0:32, :] = gr[32 * d : 32 * d + 32]
        out[d, 32:64, :] = gi[32 * d : 32 * d + 32]
        out[d, 64:80, :] = extra[d]


def fwd_call(me, tail, own, l1, tw1, m2, tj, extra):
    def whole(x):
        return pl.BlockSpec(x.shape, lambda i, m, n=x.ndim: (0,) * n)

    return pl.pallas_call(
        fwd_kernel,
        grid_spec=pltpu.PrefetchScalarGridSpec(
            num_scalar_prefetch=1,
            grid=(1,),
            in_specs=[
                whole(tail),
                whole(own),
                whole(l1),
                whole(tw1),
                whole(m2),
                pl.BlockSpec((1, 2, 512, 128), lambda i, m: (m[0], 0, 0, 0)),
                whole(extra),
            ],
            out_specs=pl.BlockSpec((16, 80, 128), lambda i, m: (0, 0, 0)),
        ),
        out_shape=jax.ShapeDtypeStruct((16, 80, 128), F32),
        compiler_params=pltpu.CompilerParams(vmem_limit_bytes=FWD_VMEM),
    )(me, tail, own, l1, tw1, m2, tj, extra)


def swap_groups(x):
    row = lax.broadcasted_iota(jnp.int32, x.shape, 0)
    lane = lax.broadcasted_iota(jnp.int32, x.shape, 1)
    n = x.shape[0]
    for t in range(3):
        d, w = 1 << t, 1 << SWAP[t]
        rb, lb = (row >> t) & 1, (lane >> SWAP[t]) & 1
        up = pltpu.roll(pltpu.roll(x, d, 0), 128 - w, 1)
        dn = pltpu.roll(pltpu.roll(x, n - d, 0), w, 1)
        x = jnp.where(rb == lb, x, jnp.where(rb == 1, up, dn))
    return x


def swap_low_bits(v):
    lane = lax.broadcasted_iota(jnp.int32, v[0].shape, 1)
    v = list(v)
    for t in range(3):
        w = 1 << t
        clear = (lane >> t) & 1 == 0
        for i in range(8):
            if not i & w:
                p, q = v[i], v[i | w]
                v[i] = jnp.where(clear, p, pltpu.roll(q, w, 1))
                v[i | w] = jnp.where(clear, pltpu.roll(p, 128 - w, 1), q)
    return v


def mix_kernel(p, w_out, sig_out):
    g = []
    for b in range(4):
        rows = [64 + 80 * (i >> 2) + 4 * (i & 3) + b for i in range(8)]
        g.append(swap_low_bits([p[pl.ds(r, 8, stride=160), :] for r in rows]))
    quarters = []
    for n in range(4):
        rows = [80 * (n + 4 * q) for q in range(4)]
        quarters.append(fft4([(p[i + 32 : i + 64, :], p[i : i + 32, :]) for i in rows]))
    for ah in range(6):
        z = [cmul(quarters[n][ah % 4], n * ah, 16) for n in range(4)]
        im, re = add(add(z[0], z[1]), add(z[2], z[3]))
        re, im = swap_groups(re), swap_groups(im)
        for b in range(4):
            at = slice(8 * b, 8 * b + 8)
            w_out[b, 8 * ah : 8 * ah + 8, :] = re[at] * g[b][ah]
            w_out[b, 48 + 8 * ah : 56 + 8 * ah, :] = im[at] * g[b][ah]
    sig = jnp.sum(g[0][6], keepdims=True) * (1.0 / 64.0)
    sig_out[...] = jnp.broadcast_to(lax.rsqrt(sig), (8, 128))


def mix_call(p):
    return pl.pallas_call(
        mix_kernel,
        out_shape=[
            jax.ShapeDtypeStruct((4, 96, 128), F32),
            jax.ShapeDtypeStruct((8, 128), F32),
        ],
        compiler_params=pltpu.CompilerParams(vmem_limit_bytes=16 << 20),
    )(p)


def inv_kernel(me, w, phi, psi, tw, twb, tw3, e1, e2, *rest):
    h_out = rest[-1]
    core = me[0] & 1
    for u in range(8):
        at = (u // 4 ^ core) * 4 + u % 4
        wr, wi = w[0, at, 0:48, :], w[0, at, 48:96, :]
        v = []
        for m in range(2):
            pc, ps = phi[0, u, 2 * m : 2 * m + 1, :], phi[0, u, 2 * m + 1 : 2 * m + 2, :]
            lane = 16 * m + u
            qc, qs = psi[0, :, lane : lane + 1], psi[0, :, lane + 8 : lane + 9]
            c, s = pc * qc - ps * qs, pc * qs + ps * qc
            v.append(jnp.concatenate([wr * c - wi * s, wr * s + wi * c]))
        vh, vl = split2(jnp.concatenate(v, 1))
        g = lax.dot_general(
            jnp.concatenate([vh, vl, vh]),
            e1[...],
            (((0,), (0,)), ((), ())),
            preferred_element_type=F32,
        )
        fc, fs, bc, bs = tw[0], tw[1], twb[u, 0:1, :], twb[u, 1:2, :]
        c, s = fc * bc - fs * bs, fc * bs + fs * bc
        zr, zi = [], []
        for m in range(2):
            gr, gi = g[128 * m : 128 * m + 128, :128], g[128 * m : 128 * m + 128, 128:]
            zr.append(gr * c - gi * s)
            zi.append(gr * s + gi * c)
        z = jnp.concatenate([jnp.concatenate(zr, 1), jnp.concatenate(zi, 1)], 0)
        zh, zl = split2(z)
        h = dot(e2[...], jnp.concatenate([zh, zl, zh], 0))
        c, s = tw3[0, :, u : u + 1], tw3[0, :, u + 8 : u + 9]
        hr, hi = h[:128], h[128:]
        h_out[:, u, 0] = (hr * c - hi * s).reshape(16, 8, 256)
        h_out[:, u, 1] = (hr * s + hi * c).reshape(16, 8, 256)


def inv_call(me, w, chips, ph, t, prev):
    count = len(chips)

    def chip(i, m):
        y, x = m[0] >> 3, (m[0] >> 1) & 3
        dy, dx = chips[0]
        for n in range(1, count):
            dy = jnp.where(i == n, chips[n][0], dy)
            dx = jnp.where(i == n, chips[n][1], dx)
        return ((y + dy) & 1) * 4 + ((x + dx) & 3)

    in_specs = [
        pl.BlockSpec((1, 8, 96, 128), lambda i, m: (i, 0, 0, 0)),
        pl.BlockSpec((1, 8, 4, 128), lambda i, m: (chip(i, m), 0, 0, 0)),
        pl.BlockSpec((1, 48, 128), lambda i, m: (chip(i, m), 0, 0)),
        pl.BlockSpec((2, 128, 128), lambda i, m: (0, 0, 0)),
        pl.BlockSpec((8, 2, 128), lambda i, m: (chip(i, m), 0, 0)),
        pl.BlockSpec((1, 128, 128), lambda i, m: (chip(i, m), 0, 0)),
        pl.BlockSpec((288, 256), lambda i, m: (0, 0)),
        pl.BlockSpec((256, 768), lambda i, m: (0, 0)),
    ]
    args = [me, w, *ph, t["tw"], t["twb"], t["tw3"], t["e1"], t["e2"]]
    alias = {}
    if prev is not None:
        in_specs.append(pl.BlockSpec(memory_space=pl.ANY))
        args.append(prev)
        alias = {9: 0}
    return pl.pallas_call(
        inv_kernel,
        grid_spec=pltpu.PrefetchScalarGridSpec(
            num_scalar_prefetch=1,
            grid=(count,),
            in_specs=in_specs,
            out_specs=pl.BlockSpec(
                (16, 8, 2, 8, 256), lambda i, m: (0, chip(i, m), 0, 0, 0)
            ),
        ),
        out_shape=jax.ShapeDtypeStruct((16, 64, 2, 8, 256), F32),
        input_output_aliases=alias,
        compiler_params=pltpu.CompilerParams(vmem_limit_bytes=INV_VMEM),
        cost_estimate=pl.CostEstimate(
            flops=count * 1_500_000_000, bytes_accessed=count * 3_000_000, transcendentals=0
        ),
    )(*args)


def cmul(x, num, den):
    num %= den
    re, im = x
    if num == 0:
        return re, im
    if 4 * num == den:
        return -im, re
    if 2 * num == den:
        return -re, -im
    if 4 * num == 3 * den:
        return im, -re
    c = float(math.cos(2 * math.pi * num / den))
    s = float(math.sin(2 * math.pi * num / den))
    if (8 * num) % den == 0:
        r = math.sqrt(0.5)
        a = r if c > 0 else -r
        b = r if s > 0 else -r
        if a == b:
            return a * (re - im), a * (re + im)
        return a * (re + im), a * (im - re)
    return re * c - im * s, re * s + im * c


def add(x, y):
    return x[0] + y[0], x[1] + y[1]


def sub(x, y):
    return x[0] - y[0], x[1] - y[1]


def fft4(x):
    p, q = add(x[0], x[2]), sub(x[0], x[2])
    r, s = add(x[1], x[3]), sub(x[1], x[3])
    s = (-s[1], s[0])
    return [add(p, r), add(q, s), sub(p, r), sub(q, s)]


def out_kernel(h, sig, out, mid):
    scale = sig[...]
    for tile, m in ((0, 0), (0, 1), (1, 0), (1, 1)):
        at = slice(128 * m, 128 * m + 128)
        for lo in range(8):
            x = [(h[tile, 8 * hi + lo, 0, :, at], h[tile, 8 * hi + lo, 1, :, at]) for hi in range(8)]
            ev, od = fft4(x[0::2]), fft4(x[1::2])
            for f in range(4):
                o = cmul(od[f], f, 8)
                for f2, v in ((f, add(ev[f], o)), (f + 4, sub(ev[f], o))):
                    v = cmul(v, lo * f2, 64)
                    mid[f2, lo, 0] = v[0]
                    mid[f2, lo, 1] = v[1]
        for f2 in range(8):
            x = [(mid[f2, lo, 0], mid[f2, lo, 1]) for lo in range(8)]
            ev, od = fft4(x[0::2]), fft4(x[1::2])
            for f in range(4):
                v = sub(ev[f], cmul(od[f], f, 8))
                power = v[0] * v[0] + v[1] * v[1]
                mag = power * lax.rsqrt(jnp.maximum(power, 1e-37)) * scale
                out[f2 + 8 * f, pl.ds(16 * tile + m, 8, stride=2), :] = mag


def out_call(h, sig):
    return pl.pallas_call(
        out_kernel,
        grid=(8,),
        in_specs=[
            pl.BlockSpec((2, 64, 2, 8, 256), lambda i: (i, 0, 0, 0, 0)),
            pl.BlockSpec((8, 128), lambda i: (0, 0)),
        ],
        out_specs=pl.BlockSpec((32, 32, 128), lambda i: (0, i, 0)),
        out_shape=jax.ShapeDtypeStruct((32, 256, 128), F32),
        scratch_shapes=[pltpu.VMEM((8, 8, 2, 8, 128), F32)],
        compiler_params=pltpu.CompilerParams(vmem_limit_bytes=OUT_VMEM),
    )(h, sig)


def place(y, x, c):
    return (y % 2 * 4 + x % 4) * 2 + c


def sent(v, dy, dx, dc):
    route = [
        (place(y, x, c), place(y + dy, x + dx, (c + dc) % 2))
        for y in range(2)
        for x in range(4)
        for c in range(2)
    ]
    return lax.ppermute(v, "tmpl", route)


def phases(chirp_slope, chirp_curve):
    row = jnp.arange(4, dtype=jnp.int32)[None, :, None]
    s = jnp.where(row < 2, chirp_slope[0], chirp_slope[1])
    c = jnp.where(row < 2, chirp_curve[0], chirp_curve[1])
    b = 64 * B1[None, None, :] + np.arange(64)[:, None, None]
    square = jnp.asarray(b * b % N, jnp.int32)
    p = (s * jnp.asarray(b, jnp.int32) + c * square - (N // 4) * (row % 2)) % N
    phi = jnp.cos(p.astype(F32) * (2 * math.pi / N))
    lane = jnp.arange(128, dtype=jnp.int32)[None, None, :]
    s = jnp.where(lane < 16, chirp_slope[0], chirp_slope[1])
    c = jnp.where(lane < 16, chirp_curve[0], chirp_curve[1])
    b0 = 8 * jnp.arange(8, dtype=jnp.int32)[:, None, None] + lane % 8
    a = jnp.arange(48, dtype=jnp.int32)[None, :, None]
    p = (a * ((s + 2 * c * b0) % 128) - 32 * (lane // 8 % 2)) % 128
    psi = jnp.cos(p.astype(F32) * (2 * math.pi / 128))
    return phi.reshape(8, 8, 4, 128), psi


def local(strain, psd_bins, psd_values, chirp_slope, chirp_curve):
    t = {k: jnp.asarray(v) for k, v in tables().items()}
    member = lax.axis_index("tmpl")
    me = member.astype(jnp.int32).reshape(1)
    own = strain.reshape(256, 128)
    count = lax.axis_size("tm")
    tail = lax.ppermute(own, "tm", [(i, i + 1) for i in range(count - 1)])

    extra = psd_call(me, psd_bins, psd_values.reshape(64, 128))
    sent_out = fwd_call(me, tail, own, t["l1"], t["tw1"], t["m2"], t["tj"], extra)
    sent_out, chirp_slope, chirp_curve = lax.optimization_barrier(
        (sent_out, chirp_slope, chirp_curve)
    )
    parts = lax.all_to_all(sent_out, "tmpl", split_axis=0, concat_axis=0, tiled=True)
    ph = phases(chirp_slope, chirp_curve)
    parts, *ph = lax.optimization_barrier((parts, *ph))
    w, scale = mix_call(parts.reshape(1280, 128))

    def work(blocks, chips, prev):
        mine = jnp.stack(blocks)
        both = jnp.concatenate([mine, sent(mine, 0, 0, 1)], 1)
        return inv_call(me, both, chips, ph, t, prev)

    up = sent(w, 1, 0, 0)
    right = sent(w, 0, 1, 0)
    left = sent(w, 0, -1, 0)
    h = work([w], [(0, 0)], None)
    up, right, left, h = lax.optimization_barrier((up, right, left, h))
    right2 = sent(jnp.concatenate([up, right[:2]]), 0, 1, 0)
    left2 = sent(jnp.concatenate([up, left[2:]]), 0, -1, 0)
    h = work([up, right, left], [(1, 0), (0, -1), (0, 1)], h)
    right2, left2, h = lax.optimization_barrier((right2, left2, h))
    right3 = sent(right2[:2], 0, 1, 0)
    left3 = sent(left2[2:4], 0, -1, 0)
    far = jnp.concatenate([right2[4:], left2[4:]])
    h = work([right2[:4], left2[:4]], [(1, -1), (1, 1)], h)
    right3, left3, h = lax.optimization_barrier((right3, left3, h))
    h = work([far], [(0, 2)], h)
    h = work([jnp.concatenate([right3, left3])], [(1, 2)], h)
    out = out_call(h, scale)
    return out.reshape(4096, 2, 128).transpose(1, 0, 2).reshape(2, 4096 * 128)


def solution(mesh):
    placed = (P("tmpl", "tm"), P(None, "tmpl"), P("tm", None), P("tmpl"), P("tmpl"))
    return jax.shard_map(
        local, mesh=mesh, in_specs=placed, out_specs=P("tmpl", "tm"), check_vma=False
    )
```

```python
import functools
import math

import jax
import jax.numpy as jnp
import ml_dtypes
import numpy as np
from jax import lax
from jax.experimental import pallas as pl
from jax.experimental.pallas import tpu as pltpu
from jax.sharding import PartitionSpec as P

N = 1 << 20
K_LOW = N // 200
BF = jnp.bfloat16
F32 = jnp.float32
INV_VMEM = 24 << 20
FWD_VMEM = 58 << 20
OUT_VMEM = 24 << 20


def halves(x):
    x = np.asarray(x, np.float32)
    hi = x.astype(ml_dtypes.bfloat16)
    lo = (x - hi.astype(np.float32)).astype(ml_dtypes.bfloat16)
    return hi, lo


def unit(num, den, sign):
    ang = (num % den) * (sign * 2.0 * math.pi / den)
    return np.cos(ang), np.sin(ang)


LANE = np.arange(128)


def bits(x, *order):
    out = 0 * x
    for b in order:
        out = 2 * out + (x >> b & 1)
    return out


B1 = bits(LANE, 2, 1, 6, 5, 4, 3, 0)
SWAP = (0, 3, 4)


@functools.lru_cache(None)
def tables():
    t = {}
    rows = np.arange(512)
    low = rows // 8 + 64 * (rows % 8)
    c, s = unit(low[:, None] * np.arange(512)[None, :], 512, -1)
    hi, lo = halves(np.concatenate([c, s]))
    t["l1"] = np.stack([hi, lo])
    c, s = unit(low[:, None] * LANE[None, :], 65536, -1)
    t["tw1"] = np.stack([c, s]).astype(np.float32)
    top = 16 * bits(LANE, 4, 3, 0) + (B1 >> 3)
    c, s = unit(LANE[:, None] * top[None, :], 128, -1)
    hi, lo = halves(np.block([[c, s], [-s, c]]))
    t["m2"] = np.concatenate([hi, hi, lo])
    q = low[:, None] + 512 * top[None, :]
    c, s = unit(np.arange(16)[:, None, None] * q[None], N, -1)
    t["tj"] = np.stack([c, s], 1).astype(np.float32)
    a = np.arange(48)
    c, s = unit(a[:, None] * LANE[None, :], 128, 1)
    hi, lo = halves(np.block([[c, s], [-s, c]]))
    t["e1"] = np.concatenate([hi, hi, lo])
    c, s = unit(LANE[:, None] * B1[None, :], 128, 1)
    hi, lo = halves(np.block([[c, -s], [s, c]]))
    t["e2"] = np.concatenate([hi, hi, lo], 1)
    c, s = unit(64 * B1[:, None] * LANE[None, :], N, 1)
    t["tw"] = np.stack([c, s]).astype(np.float32)
    c, s = unit(np.arange(64)[:, None] * LANE[None, :], N, 1)
    t["twb"] = np.stack([c, s], 1).astype(np.float32)
    c, s = unit(np.arange(64)[:, None] * LANE[None, :], 8192, 1)
    t3 = np.zeros((8, 128, 128), np.float32)
    t3[:, :, 0:8] = c.reshape(8, 8, 128).transpose(0, 2, 1)
    t3[:, :, 8:16] = s.reshape(8, 8, 128).transpose(0, 2, 1)
    t["tw3"] = t3
    return t


def split2(x):
    hi = x.astype(BF)
    lo = (x - hi.astype(F32)).astype(BF)
    return hi, lo


def dot(a, b):
    return jnp.dot(a, b, preferred_element_type=F32)


def psd_kernel(me, bins_hbm, vals_hbm, out, g, tr, bins, vals, sems):
    fetch = [
        pltpu.make_async_copy(bins_hbm, bins, sems.at[0]),
        pltpu.make_async_copy(vals_hbm, vals, sems.at[1]),
    ]
    for copy in fetch:
        copy.start()
    row = lax.broadcasted_iota(jnp.int32, (256, 128), 0)
    lane = lax.broadcasted_iota(jnp.int32, (256, 128), 1)
    k = (row & 7) * 65536 + me[0] * 4096 + (row >> 3) * 128 + lane
    ratio = jnp.maximum(k.astype(F32) / K_LOW, 1.0)
    amp = jnp.where(k >= K_LOW, jnp.exp(jnp.log(ratio) * (-7.0 / 6.0)), 0.0)
    for copy in fetch:
        copy.wait()
    v0 = vals[...]
    p0 = v0.astype(BF)
    v1 = v0 - p0.astype(F32)
    p1 = v1.astype(BF)
    p2 = (v1 - p1.astype(F32)).astype(BF)
    parts = jnp.concatenate([p0, p1, p2])
    width = 512
    low = lax.broadcasted_iota(jnp.int32, (128, width), 0)
    high = lax.broadcasted_iota(jnp.int32, (64, width), 0)
    g[...] = jnp.ones((256, 128), F32)

    def chunk(i, carry):
        at = pl.multiple_of(i * width, width)
        idx = bins[:, pl.ds(at, width)]
        for ah in range(6):
            one = idx[ah : ah + 1]
            hot = jnp.where((one & 127) == low, 1.0, 0.0).astype(BF)
            got = dot(parts, hot)
            got = got[:64] + got[64:128] + got[128:]
            got = jnp.sum(jnp.where((one >> 7) == high, got, 0.0), axis=0, keepdims=True)
            for q in range(width // 128):
                g[pl.ds(i * (width // 16) + 8 * q + ah, 1), :] = got[:, 128 * q : 128 * q + 128]
        return carry

    lax.fori_loop(0, 4096 // width, chunk, 0)
    f = amp / g[...]
    rows = (row & 7) < 6
    share = jnp.sum(jnp.where(rows, f * amp, 0.0), keepdims=True)
    full = jnp.where(rows, f * (1.0 / 1024.0), jnp.broadcast_to(share, (256, 128)))
    for half in range(2):
        tr[...] = full[128 * half : 128 * half + 128].T
        for low_bit in range(2):
            for d in range(16):
                at = 8 * half + 4 * low_bit
                src = 64 * low_bit + 4 * d
                out[d, at : at + 4, :] = tr[src : src + 4, :]


def psd_call(me, bins, vals):
    return pl.pallas_call(
        psd_kernel,
        grid_spec=pltpu.PrefetchScalarGridSpec(
            num_scalar_prefetch=1,
            grid=(1,),
            in_specs=[pl.BlockSpec(memory_space=pl.ANY)] * 2,
            out_specs=pl.BlockSpec((16, 16, 128), lambda i, m: (0, 0, 0)),
            scratch_shapes=[
                pltpu.VMEM((256, 128), F32),
                pltpu.VMEM((128, 128), F32),
                pltpu.VMEM((8, 4096), jnp.int32),
                pltpu.VMEM((64, 128), F32),
                pltpu.SemaphoreType.DMA((2,)),
            ],
        ),
        out_shape=jax.ShapeDtypeStruct((16, 16, 128), F32),
        compiler_params=pltpu.CompilerParams(vmem_limit_bytes=60 << 20),
    )(me, bins, vals)


def fwd_kernel(me, tail, own, l1, tw1, m2, tj, extra, out):
    th, tl = split2(tail[...])
    oh, ol = split2(own[...])
    xh = jnp.concatenate([th, oh])
    xl = jnp.concatenate([tl, ol])
    y = dot(l1[0], xh) + dot(l1[0], xl) + dot(l1[1], xh)
    yr, yi = y[:512], y[512:]
    c, s = tw1[0], tw1[1]
    yr, yi = yr * c - yi * s, yr * s + yi * c
    rh, rl = split2(yr)
    ih, il = split2(yi)
    f = dot(jnp.concatenate([rh, ih, rl, il, rh, ih], 1), m2[...])
    fr, fi = f[:, :128], f[:, 128:]
    c, s = tj[0, 0], tj[0, 1]
    gr, gi = fr * c - fi * s, fr * s + fi * c
    for d in range(16):
        out[d, 0:32, :] = gr[32 * d : 32 * d + 32]
        out[d, 32:64, :] = gi[32 * d : 32 * d + 32]
        out[d, 64:80, :] = extra[d]


def fwd_call(me, tail, own, l1, tw1, m2, tj, extra):
    def whole(x):
        return pl.BlockSpec(x.shape, lambda i, m, n=x.ndim: (0,) * n)

    return pl.pallas_call(
        fwd_kernel,
        grid_spec=pltpu.PrefetchScalarGridSpec(
            num_scalar_prefetch=1,
            grid=(1,),
            in_specs=[
                whole(tail),
                whole(own),
                whole(l1),
                whole(tw1),
                whole(m2),
                pl.BlockSpec((1, 2, 512, 128), lambda i, m: (m[0], 0, 0, 0)),
                whole(extra),
            ],
            out_specs=pl.BlockSpec((16, 80, 128), lambda i, m: (0, 0, 0)),
        ),
        out_shape=jax.ShapeDtypeStruct((16, 80, 128), F32),
        compiler_params=pltpu.CompilerParams(vmem_limit_bytes=FWD_VMEM),
    )(me, tail, own, l1, tw1, m2, tj, extra)


def swap_groups(x):
    row = lax.broadcasted_iota(jnp.int32, x.shape, 0)
    lane = lax.broadcasted_iota(jnp.int32, x.shape, 1)
    n = x.shape[0]
    for t in range(3):
        d, w = 1 << t, 1 << SWAP[t]
        rb, lb = (row >> t) & 1, (lane >> SWAP[t]) & 1
        up = pltpu.roll(pltpu.roll(x, d, 0), 128 - w, 1)
        dn = pltpu.roll(pltpu.roll(x, n - d, 0), w, 1)
        x = jnp.where(rb == lb, x, jnp.where(rb == 1, up, dn))
    return x


def swap_low_bits(v):
    lane = lax.broadcasted_iota(jnp.int32, v[0].shape, 1)
    v = list(v)
    for t in range(3):
        w = 1 << t
        clear = (lane >> t) & 1 == 0
        for i in range(8):
            if not i & w:
                p, q = v[i], v[i | w]
                v[i] = jnp.where(clear, p, pltpu.roll(q, w, 1))
                v[i | w] = jnp.where(clear, pltpu.roll(p, 128 - w, 1), q)
    return v


def mix_kernel(p, w_out, sig_out):
    g = []
    for b in range(4):
        rows = [64 + 80 * (i >> 2) + 4 * (i & 3) + b for i in range(8)]
        g.append(swap_low_bits([p[pl.ds(r, 8, stride=160), :] for r in rows]))
    quarters = []
    for n in range(4):
        rows = [80 * (n + 4 * q) for q in range(4)]
        quarters.append(fft4([(p[i + 32 : i + 64, :], p[i : i + 32, :]) for i in rows]))
    for ah in range(6):
        z = [cmul(quarters[n][ah % 4], n * ah, 16) for n in range(4)]
        im, re = add(add(z[0], z[1]), add(z[2], z[3]))
        re, im = swap_groups(re), swap_groups(im)
        for b in range(4):
            at = slice(8 * b, 8 * b + 8)
            w_out[b, 8 * ah : 8 * ah + 8, :] = re[at] * g[b][ah]
            w_out[b, 48 + 8 * ah : 56 + 8 * ah, :] = im[at] * g[b][ah]
    sig = jnp.sum(g[0][6], keepdims=True) * (1.0 / 64.0)
    sig_out[...] = jnp.broadcast_to(lax.rsqrt(sig), (8, 128))


def mix_call(p):
    return pl.pallas_call(
        mix_kernel,
        out_shape=[
            jax.ShapeDtypeStruct((4, 96, 128), F32),
            jax.ShapeDtypeStruct((8, 128), F32),
        ],
        compiler_params=pltpu.CompilerParams(vmem_limit_bytes=16 << 20),
    )(p)


def inv_kernel(me, w, phi, psi, tw, twb, tw3, e1, e2, *rest):
    h_out = rest[-1]
    core = me[0] & 1
    for u in range(8):
        at = (u // 4 ^ core) * 4 + u % 4
        wr, wi = w[0, at, 0:48, :], w[0, at, 48:96, :]
        v = []
        for m in range(2):
            pc, ps = phi[0, u, 2 * m : 2 * m + 1, :], phi[0, u, 2 * m + 1 : 2 * m + 2, :]
            lane = 16 * m + u
            qc, qs = psi[0, :, lane : lane + 1], psi[0, :, lane + 8 : lane + 9]
            c, s = pc * qc - ps * qs, pc * qs + ps * qc
            v.append(jnp.concatenate([wr * c - wi * s, wr * s + wi * c]))
        vh, vl = split2(jnp.concatenate(v, 1))
        g = lax.dot_general(
            jnp.concatenate([vh, vl, vh]),
            e1[...],
            (((0,), (0,)), ((), ())),
            preferred_element_type=F32,
        )
        fc, fs, bc, bs = tw[0], tw[1], twb[u, 0:1, :], twb[u, 1:2, :]
        c, s = fc * bc - fs * bs, fc * bs + fs * bc
        zr, zi = [], []
        for m in range(2):
            gr, gi = g[128 * m : 128 * m + 128, :128], g[128 * m : 128 * m + 128, 128:]
            zr.append(gr * c - gi * s)
            zi.append(gr * s + gi * c)
        z = jnp.concatenate([jnp.concatenate(zr, 1), jnp.concatenate(zi, 1)], 0)
        zh, zl = split2(z)
        h = dot(e2[...], jnp.concatenate([zh, zl, zh], 0))
        c, s = tw3[0, :, u : u + 1], tw3[0, :, u + 8 : u + 9]
        hr, hi = h[:128], h[128:]
        h_out[:, u, 0] = (hr * c - hi * s).reshape(16, 8, 256)
        h_out[:, u, 1] = (hr * s + hi * c).reshape(16, 8, 256)


def inv_call(me, w, chips, ph, t, prev):
    count = len(chips)

    def chip(i, m):
        y, x = m[0] >> 3, (m[0] >> 1) & 3
        dy, dx = chips[0]
        for n in range(1, count):
            dy = jnp.where(i == n, chips[n][0], dy)
            dx = jnp.where(i == n, chips[n][1], dx)
        return ((y + dy) & 1) * 4 + ((x + dx) & 3)

    in_specs = [
        pl.BlockSpec((1, 8, 96, 128), lambda i, m: (i, 0, 0, 0)),
        pl.BlockSpec((1, 8, 4, 128), lambda i, m: (chip(i, m), 0, 0, 0)),
        pl.BlockSpec((1, 48, 128), lambda i, m: (chip(i, m), 0, 0)),
        pl.BlockSpec((2, 128, 128), lambda i, m: (0, 0, 0)),
        pl.BlockSpec((8, 2, 128), lambda i, m: (chip(i, m), 0, 0)),
        pl.BlockSpec((1, 128, 128), lambda i, m: (chip(i, m), 0, 0)),
        pl.BlockSpec((288, 256), lambda i, m: (0, 0)),
        pl.BlockSpec((256, 768), lambda i, m: (0, 0)),
    ]
    args = [me, w, *ph, t["tw"], t["twb"], t["tw3"], t["e1"], t["e2"]]
    alias = {}
    if prev is not None:
        in_specs.append(pl.BlockSpec(memory_space=pl.ANY))
        args.append(prev)
        alias = {9: 0}
    return pl.pallas_call(
        inv_kernel,
        grid_spec=pltpu.PrefetchScalarGridSpec(
            num_scalar_prefetch=1,
            grid=(count,),
            in_specs=in_specs,
            out_specs=pl.BlockSpec(
                (16, 8, 2, 8, 256), lambda i, m: (0, chip(i, m), 0, 0, 0)
            ),
        ),
        out_shape=jax.ShapeDtypeStruct((16, 64, 2, 8, 256), F32),
        input_output_aliases=alias,
        compiler_params=pltpu.CompilerParams(vmem_limit_bytes=INV_VMEM),
        cost_estimate=pl.CostEstimate(
            flops=count * 1_500_000_000, bytes_accessed=count * 3_000_000, transcendentals=0
        ),
    )(*args)


def cmul(x, num, den):
    num %= den
    re, im = x
    if num == 0:
        return re, im
    if 4 * num == den:
        return -im, re
    if 2 * num == den:
        return -re, -im
    if 4 * num == 3 * den:
        return im, -re
    c = float(math.cos(2 * math.pi * num / den))
    s = float(math.sin(2 * math.pi * num / den))
    if (8 * num) % den == 0:
        r = math.sqrt(0.5)
        a = r if c > 0 else -r
        b = r if s > 0 else -r
        if a == b:
            return a * (re - im), a * (re + im)
        return a * (re + im), a * (im - re)
    return re * c - im * s, re * s + im * c


def add(x, y):
    return x[0] + y[0], x[1] + y[1]


def sub(x, y):
    return x[0] - y[0], x[1] - y[1]


def fft4(x):
    p, q = add(x[0], x[2]), sub(x[0], x[2])
    r, s = add(x[1], x[3]), sub(x[1], x[3])
    s = (-s[1], s[0])
    return [add(p, r), add(q, s), sub(p, r), sub(q, s)]


def out_kernel(h, sig, out, mid):
    scale = sig[...]
    for tile, m in [(n // 2, n % 2) for n in range(8)]:
        at = slice(128 * m, 128 * m + 128)
        for lo in range(8):
            x = [(h[tile, 8 * hi + lo, 0, :, at], h[tile, 8 * hi + lo, 1, :, at]) for hi in range(8)]
            ev, od = fft4(x[0::2]), fft4(x[1::2])
            for f in range(4):
                o = cmul(od[f], f, 8)
                for f2, v in ((f, add(ev[f], o)), (f + 4, sub(ev[f], o))):
                    v = cmul(v, lo * f2, 64)
                    mid[f2, lo, 0] = v[0]
                    mid[f2, lo, 1] = v[1]
        for f2 in range(8):
            x = [(mid[f2, lo, 0], mid[f2, lo, 1]) for lo in range(8)]
            ev, od = fft4(x[0::2]), fft4(x[1::2])
            for f in range(4):
                v = sub(ev[f], cmul(od[f], f, 8))
                power = v[0] * v[0] + v[1] * v[1]
                mag = power * lax.rsqrt(jnp.maximum(power, 1e-37)) * scale
                out[f2 + 8 * f, pl.ds(16 * tile + m, 8, stride=2), :] = mag


def out_call(h, sig):
    return pl.pallas_call(
        out_kernel,
        grid=(4,),
        in_specs=[
            pl.BlockSpec((4, 64, 2, 8, 256), lambda i: (i, 0, 0, 0, 0)),
            pl.BlockSpec((8, 128), lambda i: (0, 0)),
        ],
        out_specs=pl.BlockSpec((32, 64, 128), lambda i: (0, i, 0)),
        out_shape=jax.ShapeDtypeStruct((32, 256, 128), F32),
        scratch_shapes=[pltpu.VMEM((8, 8, 2, 8, 128), F32)],
        compiler_params=pltpu.CompilerParams(vmem_limit_bytes=OUT_VMEM),
    )(h, sig)


def place(y, x, c):
    return (y % 2 * 4 + x % 4) * 2 + c


def sent(v, dy, dx, dc):
    route = [
        (place(y, x, c), place(y + dy, x + dx, (c + dc) % 2))
        for y in range(2)
        for x in range(4)
        for c in range(2)
    ]
    return lax.ppermute(v, "tmpl", route)


def phases(chirp_slope, chirp_curve):
    row = jnp.arange(4, dtype=jnp.int32)[None, :, None]
    s = jnp.where(row < 2, chirp_slope[0], chirp_slope[1])
    c = jnp.where(row < 2, chirp_curve[0], chirp_curve[1])
    b = 64 * B1[None, None, :] + np.arange(64)[:, None, None]
    square = jnp.asarray(b * b % N, jnp.int32)
    p = (s * jnp.asarray(b, jnp.int32) + c * square - (N // 4) * (row % 2)) % N
    phi = jnp.cos(p.astype(F32) * (2 * math.pi / N))
    lane = jnp.arange(128, dtype=jnp.int32)[None, None, :]
    s = jnp.where(lane < 16, chirp_slope[0], chirp_slope[1])
    c = jnp.where(lane < 16, chirp_curve[0], chirp_curve[1])
    b0 = 8 * jnp.arange(8, dtype=jnp.int32)[:, None, None] + lane % 8
    a = jnp.arange(48, dtype=jnp.int32)[None, :, None]
    p = (a * ((s + 2 * c * b0) % 128) - 32 * (lane // 8 % 2)) % 128
    psi = jnp.cos(p.astype(F32) * (2 * math.pi / 128))
    return phi.reshape(8, 8, 4, 128), psi


def local(strain, psd_bins, psd_values, chirp_slope, chirp_curve):
    t = {k: jnp.asarray(v) for k, v in tables().items()}
    member = lax.axis_index("tmpl")
    me = member.astype(jnp.int32).reshape(1)
    own = strain.reshape(256, 128)
    count = lax.axis_size("tm")
    tail = lax.ppermute(own, "tm", [(i, i + 1) for i in range(count - 1)])

    extra = psd_call(me, psd_bins, psd_values.reshape(64, 128))
    sent_out = fwd_call(me, tail, own, t["l1"], t["tw1"], t["m2"], t["tj"], extra)
    sent_out, chirp_slope, chirp_curve = lax.optimization_barrier(
        (sent_out, chirp_slope, chirp_curve)
    )
    parts = lax.all_to_all(sent_out, "tmpl", split_axis=0, concat_axis=0, tiled=True)
    ph = phases(chirp_slope, chirp_curve)
    parts, *ph = lax.optimization_barrier((parts, *ph))
    w, scale = mix_call(parts.reshape(1280, 128))

    def work(blocks, chips, prev):
        mine = jnp.stack(blocks)
        both = jnp.concatenate([mine, sent(mine, 0, 0, 1)], 1)
        return inv_call(me, both, chips, ph, t, prev)

    up = sent(w, 1, 0, 0)
    right = sent(w, 0, 1, 0)
    left = sent(w, 0, -1, 0)
    h = work([w], [(0, 0)], None)
    up, right, left, h = lax.optimization_barrier((up, right, left, h))
    right2 = sent(jnp.concatenate([up, right[:2]]), 0, 1, 0)
    left2 = sent(jnp.concatenate([up, left[2:]]), 0, -1, 0)
    h = work([up, right, left], [(1, 0), (0, -1), (0, 1)], h)
    right2, left2, h = lax.optimization_barrier((right2, left2, h))
    right3 = sent(right2[:2], 0, 1, 0)
    left3 = sent(left2[2:4], 0, -1, 0)
    far = jnp.concatenate([right2[4:], left2[4:]])
    h = work([right2[:4], left2[:4]], [(1, -1), (1, 1)], h)
    right3, left3, h = lax.optimization_barrier((right3, left3, h))
    h = work([far], [(0, 2)], h)
    h = work([jnp.concatenate([right3, left3])], [(1, 2)], h)
    out = out_call(h, scale)
    return out.reshape(4096, 2, 128).transpose(1, 0, 2).reshape(2, 4096 * 128)


def solution(mesh):
    placed = (P("tmpl", "tm"), P(None, "tmpl"), P("tm", None), P("tmpl"), P("tmpl"))
    return jax.shard_map(
        local, mesh=mesh, in_specs=placed, out_specs=P("tmpl", "tm"), check_vma=False
    )
```
